256 devices in a mesh: trunk: 8 (over y_hi, x), adapter: 32 (over z, y_lo, core).
Axes of the slice: x: 4, y: 4 (y_hi: 2, y_lo: 2; y = y_hi * 2 + y_lo), z: 8, core: 2. Of those that a mesh axis runs over, the one named last changes fastest.
Arguments:
- states: bfloat16 [3072, 8192], P('trunk', 'adapter'), may hold values from -6 to 6
- opponent: int32 [3072], P('trunk'), may hold values from 0 to 511, as said below
- proj_gate: bfloat16 [8192, 20480], P('trunk', 'adapter'), may hold values from -0.0625 to 0.0625
- proj_up: bfloat16 [8192, 20480], P('trunk', 'adapter'), may hold values from -0.0625 to 0.0625
- adapter_down: bfloat16 [512, 8192, 64], P('trunk', 'adapter'), may hold values from -0.0625 to 0.0625
- adapter_up: bfloat16 [512, 64, 20480], P('trunk', None, 'adapter'), may hold values from -0.75 to 0.75
Outputs:
- hidden: bfloat16 [3072, 20480], P('trunk', 'adapter')
The draws below stay inside these ranges and needn't reach their ends.
Inputs may be any that keep to these rules, and one draw needn't show every extreme that they name: `opponent`: rows come in aligned blocks of 384. In every block, for exactly one k the opponents 64 * k to 64 * k + 63 are named by exactly 96 rows; the other 288 rows of the block are split as evenly as possible over the other values of k.
All inputs are finite; a program needn't handle non-finite values.
Results may differ from the reference program's by a relative error of at most 0.0052.
Values may be sent and summed in bfloat16 or wider, within the bound.
No kernel may reach another device: no remote copies, remote signals or barrier semaphores. Data moves between devices by JAX's collectives and lax.ppermute only.
A program may use at most 128 MiB of HBM per device.

```python
import math
import jax
import jax.numpy as jnp
from jax import lax

D = 8192
FFW = 20480
RANK = 64
OPP_T = 64
ROW_T = 384
ROWS = 3072
OPPONENTS = 512
CAP = 96


def draw_opponent(key, part):
    blocks = ROWS // ROW_T
    owners = OPPONENTS // OPP_T

    def one_block(block_key):
        key_hot, key_perm, key_within = jax.random.split(block_key, 3)
        busiest = jax.random.randint(key_hot, (), 0, owners)
        position = jnp.arange(ROW_T, dtype=jnp.int32)
        others = (position - CAP) % (owners - 1)
        others = others + (others >= busiest).astype(jnp.int32)
        owner = jnp.where(position < CAP, busiest, others)
        order = jax.random.permutation(key_perm, ROW_T)
        owner = owner[order]
        within = jax.random.randint(key_within, (ROW_T,), 0, OPP_T)
        return owner * OPP_T + within
    block_keys = jax.random.split(jax.random.fold_in(key, 17), blocks)
    return jax.vmap(one_block)(block_keys).reshape(-1).astype(jnp.int32)


def level_of(own_key, shape, cuts, low, top_value):
    gain, own = 1.0, jax.random.fold_in(own_key, 6)
    for dim, blocks in cuts:
        draws = jnp.exp(jax.random.uniform(jax.random.fold_in(own, dim), (blocks,), jnp.float32, low / len(cuts), top_value / len(cuts)))
        gain = gain * jnp.repeat(draws, shape[dim] // blocks).reshape([-1 if axis == dim else 1 for axis in range(len(shape))])
    return gain


def centred(key, shape, width, bound, shards=(), kind=jnp.bfloat16):
    entries = jax.random.normal(key, shape, jnp.float32) * width
    if len(shards) > 0:
        entries = level_of(key, shape, shards, -0.22, 0.18) * entries
    return jnp.clip(entries, min=-bound, max=bound).astype(kind)


def setup_inputs(seed: int = 0) -> dict:
    key_list = jax.random.split(jax.random.key(seed), 7)
    states = centred(key_list[0], (ROWS, D), 1.0, 6.0, ((0, 8), (1, 32)))
    opponent = draw_opponent(jax.random.fold_in(key_list[6], 71), 0)
    proj_gate = centred(key_list[2], (D, FFW), D ** -0.5, 0.0625, ((0, 8), (1, 32)))
    proj_up = centred(key_list[3], (D, FFW), D ** -0.5, 0.0625, ((0, 8), (1, 32)))
    adapter_down = centred(key_list[4], (OPPONENTS, D, RANK), D ** -0.5, 0.0625, ((0, 8), (1, 32)))
    adapter_up = centred(key_list[5], (OPPONENTS, RANK, FFW), RANK ** -0.5, 0.75, ((0, 8), (2, 32)))
    return {"states": states, "opponent": opponent, "proj_gate": proj_gate, "proj_up": proj_up, "adapter_down": adapter_down, "adapter_up": adapter_up}


def reference(states, opponent, proj_gate, proj_up, adapter_down, adapter_up):
    gate_base = jnp.dot(states, proj_gate, preferred_element_type=jnp.float32)
    up_part = jnp.dot(states, proj_up, preferred_element_type=jnp.float32)
    block = math.gcd(ROWS, 64)

    def offset_block(index):
        start = (index * block).astype(jnp.int32)
        rows_here = lax.dynamic_slice_in_dim(states, start, block, 0).astype(jnp.float32)
        ids_here = lax.dynamic_slice_in_dim(opponent, start, block, 0).astype(jnp.int32)
        down_here = adapter_down[ids_here].astype(jnp.float32)
        lowrank = jnp.einsum("rd,rdk->rk", rows_here, down_here)
        lowrank_half = lowrank.astype(jnp.bfloat16)
        lowrank_half = lax.optimization_barrier(lowrank_half)
        up_here = adapter_up[ids_here].astype(jnp.float32)
        offset = jnp.einsum("rk,rkh->rh", lowrank_half.astype(jnp.float32), up_here)
        return offset.astype(jnp.bfloat16)

    offsets = lax.map(offset_block, jnp.arange(ROWS // block, dtype=jnp.int32))
    offsets = offsets.reshape(ROWS, FFW)
    hidden = jax.nn.silu(gate_base + offsets.astype(jnp.float32)) * up_part
    return hidden.astype(jnp.bfloat16)
```

```python
import jax
import jax.numpy as jnp
from jax import lax
from jax.sharding import Mesh, PartitionSpec as P

TRUNK = ("yh", "x")
ADAPTER = ("z", "yl", "c")
SWAP = [(0, 1), (1, 0)]


def shift(size, step):
    return [(i, (i + step) % size) for i in range(size)]


def gather_states(states):
    rows, width = states.shape
    nx, nz = lax.axis_size("x"), lax.axis_size("z")
    nh = nz // nx
    swap_pairs = [
        (xs * nz + h * nx + xd, xd * nz + h * nx + xs)
        for xs in range(nx)
        for h in range(nh)
        for xd in range(nx)
    ]
    mine = lax.ppermute(states, ("x", "z"), swap_pairs)
    other = lax.ppermute(mine, "yl", SWAP)
    low = lax.axis_index("yl") == 0
    first = jnp.where(low, mine, other)
    second = jnp.where(low, other, mine)
    pair = jnp.concatenate([first, second], axis=1)
    core = lax.axis_index("c")
    z = lax.axis_index("z")
    yh = lax.axis_index("yh")
    whole = jnp.zeros((nx * rows, nh * 4 * width), states.dtype)

    def put(whole, piece, offset, of_core, parts):
        at = lax.rem(z + offset + nz, nz)
        h, row = at // nx, lax.rem(at, nx)
        place = jnp.where(h == yh, 0, 1)
        for n, part in enumerate(parts):
            column = place * (4 * width) + part * 2 * width + of_core * width
            whole = lax.dynamic_update_slice(
                whole, piece[:, n * width : (n + 1) * width], (row * rows, column)
            )
        return whole

    def both(whole, piece, offset, parts):
        whole = put(whole, piece, offset, core, parts)
        twin = lax.ppermute(piece, "c", SWAP)
        return put(whole, twin, offset, 1 - core, parts)

    whole = both(whole, pair, 0, (0, 1))
    forward = backward = pair
    for step in range(1, 4):
        forward = lax.ppermute(forward, "z", shift(nz, 1))
        backward = lax.ppermute(backward, "z", shift(nz, -1))
        whole = both(whole, forward, -step, (0, 1))
        whole = both(whole, backward, step, (0, 1))
    forward = lax.ppermute(forward[:, :width], "z", shift(nz, 1))
    backward = lax.ppermute(backward[:, width:], "z", shift(nz, -1))
    whole = both(whole, forward, -4, (0,))
    whole = both(whole, backward, 4, (1,))
    return whole


def reduce_rank(partial):
    slots, rank = partial.shape
    n = lax.axis_size(ADAPTER)
    parts = lax.all_to_all(
        partial.reshape(n, slots // n, rank), ADAPTER, split_axis=0, concat_axis=0, tiled=True
    )
    mine = jnp.sum(parts, axis=0).astype(jnp.bfloat16)
    spread = jnp.broadcast_to(mine[None], (n, slots // n, rank))
    return lax.all_to_all(
        spread, ADAPTER, split_axis=0, concat_axis=0, tiled=True
    ).reshape(slots, rank)


def on_device(states, opponent, proj_gate, proj_up, adapter_down, adapter_up):
    rows, width = states.shape
    hidden = proj_gate.shape[1]
    nx, nh = lax.axis_size("x"), lax.axis_size("yh")
    owners = nx * nh
    per_owner = adapter_down.shape[0]
    capacity = 2 * rows // owners
    slots = owners * capacity
    x, yh = lax.axis_index("x"), lax.axis_index("yh")
    me = yh * nx + x

    up_other = lax.ppermute(proj_up, "yh", SWAP)
    gate_other = lax.ppermute(proj_gate, "yh", SWAP)

    ids = lax.all_to_all(
        jnp.broadcast_to(opponent[None, :], (owners, rows)), TRUNK, 0, 0, tiled=True
    )

    def slot_of(names):
        target = names // per_owner
        choose = (target[:, None] == jnp.arange(owners, dtype=jnp.int32)[None, :])
        before = (
            jnp.arange(rows, dtype=jnp.int32)[:, None] > jnp.arange(rows, dtype=jnp.int32)[None, :]
        )
        count = jnp.dot(
            before.astype(jnp.bfloat16),
            choose.astype(jnp.bfloat16),
            preferred_element_type=jnp.float32,
        ).astype(jnp.int32)
        position = jnp.sum(jnp.where(choose, count, 0), axis=1)
        return target, position

    target, position = slot_of(opponent)
    placed = (target * capacity + position)[None, :] == jnp.arange(slots, dtype=jnp.int32)[:, None]
    send = jnp.dot(
        placed.astype(jnp.bfloat16), states, preferred_element_type=jnp.float32
    ).astype(jnp.bfloat16)
    recv = lax.all_to_all(
        send.reshape(owners, capacity, width), TRUNK, 0, 0, tiled=True
    ).reshape(slots, width)

    targets, positions = jax.vmap(slot_of)(ids)
    seat = jnp.arange(capacity, dtype=jnp.int32)
    mine = (targets[:, None, :] == me) & (positions[:, None, :] == seat[None, :, None])
    local = jnp.sum(jnp.where(mine, (ids % per_owner + 1)[:, None, :], 0), axis=2) - 1
    local = local.reshape(slots)
    select = local[:, None] == jnp.arange(per_owner, dtype=jnp.int32)[None, :]
    products = jnp.einsum("sd,jdk->sjk", recv, adapter_down, preferred_element_type=jnp.float32)
    partial_rank = jnp.sum(jnp.where(select[:, :, None], products, 0.0), axis=1)
    rank_half = reduce_rank(partial_rank)
    spread = jnp.where(select[:, :, None], rank_half[:, None, :], jnp.zeros((), jnp.bfloat16))
    offsets = jnp.einsum(
        "sjk,jkh->sh", spread, adapter_up, preferred_element_type=jnp.float32
    ).astype(jnp.bfloat16)
    offsets = offsets.reshape(nh, nx, capacity, hidden)
    kept = lax.dynamic_index_in_dim(offsets, yh, 0, keepdims=False)
    given = lax.dynamic_index_in_dim(offsets, 1 - yh, 0, keepdims=False)
    taken = lax.ppermute(given, "yh", SWAP)

    half_t = lax.dynamic_slice_in_dim(targets, yh * nx, nx, 0)
    half_p = lax.dynamic_slice_in_dim(positions, yh * nx, nx, 0)

    def place(owner):
        return (
            (half_t[:, :, None] == owner) & (half_p[:, :, None] == seat[None, None, :])
        ).astype(jnp.bfloat16)

    other = (1 - yh) * nx + x
    seats = jnp.concatenate([place(me), place(other)], axis=2)
    filled = jnp.concatenate([kept, taken], axis=1)
    offset = jnp.einsum("brs,bsh->brh", seats, filled, preferred_element_type=jnp.float32)

    whole = gather_states(states)
    depth = proj_up.shape[0]
    own, far = whole[:, :depth], whole[:, depth:]

    def partial(weights, weights_other):
        return jnp.dot(own, weights, preferred_element_type=jnp.float32) + jnp.dot(
            far, weights_other, preferred_element_type=jnp.float32
        )

    def scatter(values):
        parts = lax.all_to_all(
            values.astype(jnp.bfloat16).reshape(nx, rows, hidden), "x", 0, 0, tiled=True
        )
        return jnp.sum(parts.astype(jnp.float32), axis=0)

    up_sum = scatter(partial(proj_up, up_other))
    gate_sum = scatter(partial(proj_gate, gate_other) + offset.reshape(nx * rows, hidden))
    return (jax.nn.silu(gate_sum) * up_sum).astype(jnp.bfloat16)


def solution(mesh):
    fine = Mesh(mesh.devices.reshape(2, 4, 8, 2, 2), TRUNK + ADAPTER)
    placed = (
        P(TRUNK, ADAPTER),
        P(TRUNK),
        P(TRUNK, ADAPTER),
        P(TRUNK, ADAPTER),
        P(TRUNK, ADAPTER, None),
        P(TRUNK, None, ADAPTER),
    )
    return jax.shard_map(
        on_device, mesh=fine, in_specs=placed, out_specs=P(TRUNK, ADAPTER), check_vma=False
    )
```

```python
import functools

import jax
import jax.numpy as jnp
from jax import lax
from jax.experimental import pallas as pl
from jax.experimental.pallas import tpu as pltpu
from jax.sharding import Mesh, PartitionSpec as P

TRUNK = ("yh", "x")
ADAPTER = ("z", "yl", "c")
SWAP = [(0, 1), (1, 0)]
NX, NZ = 4, 8
LANES = 128
VMEM_SPEC = pl.BlockSpec(memory_space=pltpu.VMEM)
COST = pl.CostEstimate(flops=8 * 10**9, bytes_accessed=16 * 2**20, transcendentals=0)


def after(value, *others):
    return lax.optimization_barrier((value, others))[0]


def start_pairs(flip):
    pairs = []
    for xs in range(NX):
        for h in range(2):
            for xd in range(NX):
                for yl in range(2):
                    source = (xs * NZ + h * NX + xd) * 2 + yl
                    z = 2 * ((xs - xd) % NX) + h
                    pairs.append((source, (xd * NZ + z) * 2 + (yl ^ flip)))
    return pairs


def finish_pairs(step):
    pairs = []
    for x in range(NX):
        for z in range(NZ):
            turn = 2 * (z % 2) - 1
            to = (x + z // 2 + (0, turn, -turn, 2)[step]) % NX
            pairs.append((x * NZ + z, to * NZ + z))
    return pairs


def gather_ring(mine, other):
    width = mine.shape[1]
    own = jnp.concatenate([mine, other], axis=1)
    odd = [(i, (i - 1 + 2 * (i % 2)) % NZ) for i in range(NZ)]
    even = [(i, (i + 1 - 2 * (i % 2)) % NZ) for i in range(NZ)]
    p1, q1 = lax.ppermute(own, "z", odd), lax.ppermute(own, "z", even)
    p2, q2 = lax.ppermute(q1, "z", odd), lax.ppermute(p1, "z", even)
    p3, q3 = lax.ppermute(q2, "z", odd), lax.ppermute(p2, "z", even)
    last = (
        lax.ppermute(q3[:, :width], "z", odd),
        lax.ppermute(p3[:, width:], "z", even),
    )

    def twin(piece):
        return tuple(lax.ppermute(part, "c", SWAP) for part in piece)

    def group(near, far):
        return (near, twin(near), far, twin(far))

    groups = [
        group((own,), (q1,)),
        group((p2,), (p1,)),
        group((q2,), (q3,)),
        group(last, (p3,)),
    ]
    return groups, (p1, p2, p3)


def multiply_kernel(shape, n_far, flags, *refs):
    count = len(shape)
    n_rows = sum(parts for group in shape for parts in group)
    row_refs, refs = refs[:n_rows], refs[n_rows:]
    own_ref, far_refs, refs = refs[0], refs[1 : 1 + n_far], refs[1 + n_far :]
    out_refs, (lhs, rhs, lhs_sems, rhs_sems) = refs[:count], refs[count:]
    side, yl, core = flags[0], flags[1], flags[2]
    depth = own_ref.shape[0]
    width = depth // 4
    weights = []
    for n in range(8):
        far, source_yl, source_core = n // 4, (n // 2) % 2, n % 2
        block = side if far == 0 else 1 - side
        c = jnp.where(core == source_core, 0, 1)
        y = jnp.where(yl == source_yl, 0, 1)
        to = pl.multiple_of(block * depth + (c * 2 + y) * width, width)
        if far:
            first = (n % 4) * width
            ref = far_refs[first * n_far // depth]
            ref = ref.at[pl.ds(first % (depth // n_far), width), :]
        else:
            ref = own_ref.at[pl.ds((n % 4) * width, width), :]
        weights.append(pltpu.make_async_copy(ref, rhs.at[pl.ds(to, width), :], rhs_sems.at[n]))
    for copy in weights:
        copy.start()
    index = 0
    waits = []
    for group, pieces in enumerate(shape):
        copies = []
        for piece, parts in enumerate(pieces):
            for part in range(parts):
                span = 2 * width // parts
                copies.append(
                    pltpu.make_async_copy(
                        row_refs[index],
                        lhs.at[group, :, pl.ds(piece * 2 * width + part * span, span)],
                        lhs_sems.at[index],
                    )
                )
                index += 1
        for copy in copies:
            copy.start()
        waits.append(copies)
    for copy in weights:
        copy.wait()
    for group, copies in enumerate(waits):
        for copy in copies:
            copy.wait()
        out_refs[group][...] = jnp.dot(
            lhs[group], rhs[...], preferred_element_type=jnp.float32
        ).astype(jnp.bfloat16)


def multiply(groups, weights, weights_far, flags, *others):
    shape = [[len(piece) for piece in group] for group in groups]
    arrays = [part for group in groups for piece in group for part in piece]
    count, rows = len(groups), arrays[0].shape[0]
    depth, hidden = weights.shape
    n_far = len(weights_far)
    anywhere = pl.BlockSpec(memory_space=pl.ANY)
    return pl.pallas_call(
        functools.partial(multiply_kernel, shape, n_far),
        out_shape=[jax.ShapeDtypeStruct((rows, hidden), jnp.bfloat16)] * count,
        in_specs=[pl.BlockSpec(memory_space=pltpu.SMEM)]
        + [anywhere] * (len(arrays) + 1 + n_far),
        out_specs=[VMEM_SPEC] * count,
        scratch_shapes=[
            pltpu.VMEM((count, rows, 2 * depth), jnp.bfloat16),
            pltpu.VMEM((2 * depth, hidden), jnp.bfloat16),
            pltpu.SemaphoreType.DMA((len(arrays),)),
            pltpu.SemaphoreType.DMA((8,)),
        ],
        compiler_params=pltpu.CompilerParams(vmem_limit_bytes=14 * 2**20),
        cost_estimate=COST,
        name="multiply",
    )(after(flags, *others), *arrays, weights, *weights_far)


def names_of(recv_ref, tile, rows):
    return recv_ref[pl.ds(tile * rows, rows), 256:].astype(jnp.float32)


def opponent_of(lanes, first, rank):
    return (first + 1 + lax.broadcasted_iota(jnp.int32, (1, lanes), 1) // rank).astype(jnp.float32)


def down_kernel(recv_ref, down_ref, out_ref, total):
    slots, rank, width = recv_ref.shape[0], 64, 256
    tiles = 3
    rows = slots // tiles
    total[...] = jnp.zeros_like(total)

    def step(chunk, carry):
        maps = down_ref[pl.ds(pl.multiple_of(chunk * 4 * rank, 4 * rank), 4 * rank), :]
        for tile in range(tiles):
            at = pl.ds(tile * rows, rows)
            product = lax.dot_general(
                recv_ref[at, :width], maps, (((1,), (1,)), ((), ())),
                preferred_element_type=jnp.float32,
            )
            names = names_of(recv_ref, tile, rows)
            first = names == opponent_of(LANES, chunk * 4, rank)
            second = names == opponent_of(LANES, chunk * 4 + 2, rank)
            total[at, :] += jnp.where(first, product[:, :LANES], 0.0) + jnp.where(
                second, product[:, LANES:], 0.0
            )
        return carry

    lax.fori_loop(0, down_ref.shape[0] // (4 * rank), step, 0)
    both = total[...] + pltpu.roll(total[...], rank, 1)
    n = out_ref.shape[0]
    low = both[: 16 * n].reshape(n, 16, LANES)
    high = both[16 * n :].reshape(n, 8, LANES)
    left = lax.broadcasted_iota(jnp.int32, (1, 1, LANES), 2) < rank
    out_ref[:, :8, :] = jnp.where(left, low[:, :8], high)
    out_ref[:, 8:, :] = jnp.where(left, low[:, 8:], 0.0)


def up_kernel(rank_ref, recv_ref, up_ref, out_ref, whole, spread):
    slots, rank = recv_ref.shape[0], 64
    n = rank_ref.shape[0]
    packed = rank_ref[...].astype(jnp.float32)
    left = lax.broadcasted_iota(jnp.int32, (1, LANES), 1) < rank
    low = packed.reshape(n * 16, LANES)
    high = packed[:, :8].reshape(n * 8, LANES)
    whole[: n * 16, :] = jnp.where(left, low, pltpu.roll(low, rank, 1))
    whole[n * 16 :, :] = jnp.where(left, pltpu.roll(high, rank, 1), high)
    tiles = 3
    rows = slots // tiles

    def step(tile, carry):
        at = pl.ds(pl.multiple_of(tile * rows, rows), rows)
        names = recv_ref[at, 256:].astype(jnp.float32)
        values = whole[at, :]
        for pair in range(up_ref.shape[0] // LANES):
            mine = names == opponent_of(LANES, pair * 2, rank)
            spread[:, pair * LANES : (pair + 1) * LANES] = jnp.where(mine, values, 0.0).astype(
                jnp.bfloat16
            )
        out_ref[at, :] = jnp.dot(
            spread[...], up_ref[...], preferred_element_type=jnp.float32
        ).astype(out_ref.dtype)
        return carry

    lax.fori_loop(0, tiles, step, 0)


def on_device(states, opponent, proj_gate, proj_up, adapter_down, adapter_up):
    rows, width = states.shape
    hidden = proj_gate.shape[1]
    owners = lax.axis_size(TRUNK)
    n_adapter = lax.axis_size(ADAPTER)
    per_owner, _, rank = adapter_down.shape
    capacity = 2 * rows // owners
    slots = owners * capacity
    side = jnp.where(lax.axis_index("z") % 2 == lax.axis_index("yh"), 0, 1)
    flags = jnp.stack([side, lax.axis_index("yl"), lax.axis_index("c")]).astype(jnp.int32)

    mine = lax.ppermute(states, ("x", "z", "yl"), start_pairs(0))
    other = lax.ppermute(states, ("x", "z", "yl"), start_pairs(1))
    cut = proj_up.shape[0] // 2
    up_far = [lax.ppermute(part, "yh", SWAP) for part in (proj_up[:cut], proj_up[cut:])]

    target = opponent // per_owner
    choose = target[:, None] == jnp.arange(owners, dtype=jnp.int32)[None, :]
    count = jnp.arange(rows, dtype=jnp.int32)
    before = (count[:, None] > count[None, :]).astype(jnp.bfloat16)
    ahead = jnp.dot(before, choose.astype(jnp.bfloat16), preferred_element_type=jnp.float32)
    position = jnp.sum(jnp.where(choose, ahead, 0.0), axis=1).astype(jnp.int32)
    placed = (
        (target * capacity + position)[None, :] == jnp.arange(slots, dtype=jnp.int32)[:, None]
    ).astype(jnp.bfloat16)
    number = jnp.broadcast_to((opponent % per_owner + 1)[:, None], (rows, LANES))
    payload = jnp.concatenate([states, number.astype(jnp.bfloat16)], axis=1)
    send = jnp.dot(placed, payload, preferred_element_type=jnp.float32).astype(jnp.bfloat16)
    recv = lax.all_to_all(
        send.reshape(owners, capacity, width + LANES), TRUNK, 0, 0, tiled=True
    ).reshape(slots, width + LANES)

    groups, steps = gather_ring(*after((mine, other), send))
    gate_far = [
        lax.ppermute(after(part, before), "yh", SWAP)
        for part, before in ((proj_gate[:cut], steps[0]), (proj_gate[cut:], steps[1]))
    ]

    partial_rank = pl.pallas_call(
        down_kernel,
        out_shape=jax.ShapeDtypeStruct((n_adapter, 16, LANES), jnp.float32),
        in_specs=[VMEM_SPEC] * 2,
        out_specs=VMEM_SPEC,
        scratch_shapes=[pltpu.VMEM((slots, LANES), jnp.float32)],
        compiler_params=pltpu.CompilerParams(vmem_limit_bytes=14 * 2**20),
        cost_estimate=COST,
        name="down",
    )(after(recv, up_far[0], steps[0]), jnp.transpose(adapter_down, (0, 2, 1)).reshape(per_owner * rank, width))
    rank_parts = lax.all_to_all(partial_rank, ADAPTER, 0, 0, tiled=True)
    rank_sum = jnp.sum(rank_parts, axis=0).astype(jnp.bfloat16)
    rank_half = lax.all_to_all(
        jnp.broadcast_to(rank_sum[None], (n_adapter, 16, LANES)), ADAPTER, 0, 0, tiled=True
    )

    ups, gates, last = [], [], []

    def finish(some, sums, weights, weights_far, *others):
        parts = multiply([groups[i] for i in some], weights, weights_far, flags, *others, *last)
        last[:] = [parts[0]]
        for at, i in enumerate(some):
            sums.append(lax.ppermute(parts[at], ("x", "z"), finish_pairs(i)))

    finish([0, 1], ups, proj_up, up_far, rank_sum)
    offsets = pl.pallas_call(
        up_kernel,
        out_shape=jax.ShapeDtypeStruct((slots, hidden), jnp.bfloat16),
        in_specs=[VMEM_SPEC] * 3,
        out_specs=VMEM_SPEC,
        scratch_shapes=[
            pltpu.VMEM((slots, LANES), jnp.float32),
            pltpu.VMEM((slots // 3, per_owner * rank), jnp.bfloat16),
        ],
        compiler_params=pltpu.CompilerParams(vmem_limit_bytes=18 * 2**20),
        cost_estimate=COST,
        name="up",
    )(after(rank_half, last[0], gate_far[0]), recv, adapter_up.reshape(per_owner * rank, hidden))
    returned = lax.all_to_all(
        offsets.reshape(owners, capacity, hidden), TRUNK, 0, 0, tiled=True
    ).reshape(slots, hidden)
    finish([2, 3], ups, proj_up, up_far, offsets)
    finish([0, 1], gates, proj_gate, gate_far, ups[0])
    finish([2, 3], gates, proj_gate, gate_far, ups[1])
    offset = lax.dot_general(
        placed, returned, (((0,), (0,)), ((), ())), preferred_element_type=jnp.float32
    )
    up_sum = functools.reduce(jnp.add, [value.astype(jnp.float32) for value in ups])
    gate_sum = functools.reduce(jnp.add, [value.astype(jnp.float32) for value in gates])
    return (jax.nn.silu(gate_sum + offset) * up_sum).astype(jnp.bfloat16)


def solution(mesh):
    fine = Mesh(mesh.devices.reshape(2, NX, NZ, 2, 2), TRUNK + ADAPTER)
    placed = (
        P(TRUNK, ADAPTER),
        P(TRUNK),
        P(TRUNK, ADAPTER),
        P(TRUNK, ADAPTER),
        P(TRUNK, ADAPTER, None),
        P(TRUNK, None, ADAPTER),
    )
    return jax.shard_map(
        on_device, mesh=fine, in_specs=placed, out_specs=P(TRUNK, ADAPTER), check_vma=False
    )
```

```python
import jax
import jax.numpy as jnp
from jax import lax
from jax.experimental import pallas as pl
from jax.experimental.pallas import tpu as pltpu
from jax.sharding import Mesh, PartitionSpec as P

TRUNK = ("yh", "x")
ADAPTER = ("z", "yl", "c")
SWAP = [(0, 1), (1, 0)]
NX, NZ = 4, 8
LANES = 128
HBM_SPEC = pl.BlockSpec(memory_space=pltpu.HBM)
VMEM_SPEC = pl.BlockSpec(memory_space=pltpu.VMEM)
COST = pl.CostEstimate(flops=8 * 10**9, bytes_accessed=16 * 2**20, transcendentals=0)


def after(value, *others):
    return lax.optimization_barrier((value, others))[0]


def start_pairs(flip):
    pairs = []
    for xs in range(NX):
        for h in range(2):
            for xd in range(NX):
                for yl in range(2):
                    source = (xs * NZ + h * NX + xd) * 2 + yl
                    pairs.append((source, (xd * NZ + h * NX + xs) * 2 + (yl ^ flip)))
    return pairs


def multiply_kernel(flags, rows_ref, own_ref, far_low, far_high, *refs):
    out_ref, lhs, rhs, lhs_sems, rhs_sems = refs[-5:]
    yh, yl = flags[0], flags[1]
    depth = own_ref.shape[0]
    width = depth // 4
    weights = []
    for n in range(8):
        block = yh if n < 4 else 1 - yh
        ref = own_ref if n < 4 else (far_low if n < 6 else far_high)
        first = (n % 4 if n < 4 else n % 2) * width
        source_yl, source_core = (n // 2) % 2, n % 2
        y = jnp.where(yl == source_yl, 0, 1)
        to = pl.multiple_of(block * depth + (source_core * 2 + y) * width, width)
        weights.append(
            pltpu.make_async_copy(
                ref.at[pl.ds(first, width), :],
                rhs.at[pl.ds(to, width), :],
                rhs_sems.at[n],
            )
        )
    for copy in weights:
        copy.start()
    rows = [
        [
            pltpu.make_async_copy(
                rows_ref.at[(h * NX + x) * 2 + core],
                lhs.at[x, :, pl.ds((h * 2 + core) * 2 * width, 2 * width)],
                lhs_sems.at[x, h * 2 + core],
            )
            for h in range(2)
            for core in range(2)
        ]
        for x in range(NX)
    ]
    for copies in rows:
        for copy in copies:
            copy.start()
    for copy in weights:
        copy.wait()
    for x, copies in enumerate(rows):
        for copy in copies:
            copy.wait()
        out_ref[x] = jnp.dot(
            lhs[x], rhs[...], preferred_element_type=jnp.float32
        ).astype(jnp.bfloat16)


def multiply(rows, weights, weights_far, flags, *others):
    count = rows.shape[1]
    depth, hidden = weights.shape
    return pl.pallas_call(
        multiply_kernel,
        out_shape=jax.ShapeDtypeStruct((NX, count, hidden), jnp.bfloat16),
        in_specs=[pl.BlockSpec(memory_space=pltpu.SMEM)] + [HBM_SPEC] * (4 + len(others)),
        out_specs=VMEM_SPEC,
        scratch_shapes=[
            pltpu.VMEM((NX, count, 2 * depth), jnp.bfloat16),
            pltpu.VMEM((2 * depth, hidden), jnp.bfloat16),
            pltpu.SemaphoreType.DMA((NX, 4)),
            pltpu.SemaphoreType.DMA((8,)),
        ],
        compiler_params=pltpu.CompilerParams(vmem_limit_bytes=56 * 2**20),
        cost_estimate=COST,
        name="multiply",
    )(flags, rows, weights, *weights_far, *others)


def names_of(recv_ref, tile, rows):
    return recv_ref[pl.ds(tile * rows, rows), 256:].astype(jnp.float32)


def opponent_of(lanes, first, rank):
    return (first + 1 + lax.broadcasted_iota(jnp.int32, (1, lanes), 1) // rank).astype(jnp.float32)


def down_kernel(recv_ref, down_ref, _, out_ref, total):
    slots, rank, width = recv_ref.shape[0], 64, 256
    tiles = 3
    rows = slots // tiles
    total[...] = jnp.zeros_like(total)

    def step(chunk, carry):
        maps = down_ref[pl.ds(pl.multiple_of(chunk * 4 * rank, 4 * rank), 4 * rank), :]
        for tile in range(tiles):
            at = pl.ds(tile * rows, rows)
            product = lax.dot_general(
                recv_ref[at, :width], maps, (((1,), (1,)), ((), ())),
                preferred_element_type=jnp.float32,
            )
            names = names_of(recv_ref, tile, rows)
            first = names == opponent_of(LANES, chunk * 4, rank)
            second = names == opponent_of(LANES, chunk * 4 + 2, rank)
            total[at, :] += jnp.where(first, product[:, :LANES], 0.0) + jnp.where(
                second, product[:, LANES:], 0.0
            )
        return carry

    lax.fori_loop(0, down_ref.shape[0] // (4 * rank), step, 0)
    both = total[...] + pltpu.roll(total[...], rank, 1)
    n = out_ref.shape[0]
    low = both[: 16 * n].reshape(n, 16, LANES)
    high = both[16 * n :].reshape(n, 8, LANES)
    left = lax.broadcasted_iota(jnp.int32, (1, 1, LANES), 2) < rank
    out_ref[:, :8, :] = jnp.where(left, low[:, :8], high)
    out_ref[:, 8:, :] = jnp.where(left, low[:, 8:], 0.0)


def sum_kernel(parts_ref, _, out_ref):
    total = jnp.sum(parts_ref[...], axis=0).astype(jnp.bfloat16)
    out_ref[...] = jnp.broadcast_to(total[None], out_ref.shape)


def up_kernel(rank_ref, recv_ref, up_ref, _, __, out_ref, whole, spread):
    slots, rank = recv_ref.shape[0], 64
    n = rank_ref.shape[0]
    packed = rank_ref[...].astype(jnp.float32)
    left = lax.broadcasted_iota(jnp.int32, (1, LANES), 1) < rank
    low = packed.reshape(n * 16, LANES)
    high = packed[:, :8].reshape(n * 8, LANES)
    whole[: n * 16, :] = jnp.where(left, low, pltpu.roll(low, rank, 1))
    whole[n * 16 :, :] = jnp.where(left, pltpu.roll(high, rank, 1), high)
    tiles = 3
    rows = slots // tiles

    def step(tile, carry):
        at = pl.ds(pl.multiple_of(tile * rows, rows), rows)
        names = recv_ref[at, 256:].astype(jnp.float32)
        values = whole[at, :]
        for pair in range(up_ref.shape[0] // LANES):
            mine = names == opponent_of(LANES, pair * 2, rank)
            spread[:, pair * LANES : (pair + 1) * LANES] = jnp.where(mine, values, 0.0).astype(
                jnp.bfloat16
            )
        out_ref[at, :] = jnp.dot(
            spread[...], up_ref[...], preferred_element_type=jnp.float32
        ).astype(out_ref.dtype)
        return carry

    lax.fori_loop(0, tiles, step, 0)


def on_device(states, opponent, proj_gate, proj_up, adapter_down, adapter_up):
    rows, width = states.shape
    hidden = proj_gate.shape[1]
    owners = lax.axis_size(TRUNK)
    n_adapter = lax.axis_size(ADAPTER)
    per_owner, _, rank = adapter_down.shape
    capacity = 2 * rows // owners
    slots = owners * capacity
    flags = jnp.stack([lax.axis_index("yh"), lax.axis_index("yl")]).astype(jnp.int32)

    mine = lax.ppermute(states, ("x", "z", "yl"), start_pairs(0))
    other = lax.ppermute(states, ("x", "z", "yl"), start_pairs(1))
    cut = proj_up.shape[0] // 2
    up_far, gate_far = (
        [lax.ppermute(part, "yh", SWAP) for part in (weights[:cut], weights[cut:])]
        for weights in (proj_up, proj_gate)
    )

    target = opponent // per_owner
    choose = target[:, None] == jnp.arange(owners, dtype=jnp.int32)[None, :]
    count = jnp.arange(rows, dtype=jnp.int32)
    before = (count[:, None] > count[None, :]).astype(jnp.bfloat16)
    ahead = jnp.dot(before, choose.astype(jnp.bfloat16), preferred_element_type=jnp.float32)
    position = jnp.sum(jnp.where(choose, ahead, 0.0), axis=1).astype(jnp.int32)
    placed = (
        (target * capacity + position)[None, :] == jnp.arange(slots, dtype=jnp.int32)[:, None]
    ).astype(jnp.bfloat16)
    number = jnp.broadcast_to((opponent % per_owner + 1)[:, None], (rows, LANES))
    payload = jnp.concatenate([states, number.astype(jnp.bfloat16)], axis=1)
    send = jnp.dot(placed, payload, preferred_element_type=jnp.float32).astype(jnp.bfloat16)
    recv = lax.all_to_all(
        send.reshape(owners, capacity, width + LANES), TRUNK, 0, 0, tiled=True
    ).reshape(slots, width + LANES)

    mine, other = after((mine, other), send)
    gathered = lax.all_gather(jnp.concatenate([mine, other], axis=1), ("z", "c"), axis=0)

    partial_rank = pl.pallas_call(
        down_kernel,
        out_shape=jax.ShapeDtypeStruct((n_adapter, 16, LANES), jnp.float32),
        in_specs=[VMEM_SPEC] * 2 + [HBM_SPEC],
        out_specs=VMEM_SPEC,
        scratch_shapes=[pltpu.VMEM((slots, LANES), jnp.float32)],
        compiler_params=pltpu.CompilerParams(vmem_limit_bytes=14 * 2**20),
        cost_estimate=COST,
        name="down",
    )(recv, jnp.transpose(adapter_down, (0, 2, 1)).reshape(per_owner * rank, width), up_far[0])
    rank_parts = lax.all_to_all(partial_rank, ADAPTER, 0, 0, tiled=True)
    rank_sum = pl.pallas_call(
        sum_kernel,
        out_shape=jax.ShapeDtypeStruct((n_adapter, 16, LANES), jnp.bfloat16),
        in_specs=[VMEM_SPEC, HBM_SPEC],
        out_specs=VMEM_SPEC,
        cost_estimate=COST,
        name="sum",
    )(rank_parts, up_far[1])
    rank_half = lax.all_to_all(rank_sum, ADAPTER, 0, 0, tiled=True)
    ups = multiply(gathered, proj_up, up_far, flags, rank_half, gate_far[0])
    up_sum = lax.psum_scatter(ups, "x", scatter_dimension=0, tiled=False)
    offsets = pl.pallas_call(
        up_kernel,
        out_shape=jax.ShapeDtypeStruct((slots, hidden), jnp.bfloat16),
        in_specs=[VMEM_SPEC] * 3 + [HBM_SPEC] * 2,
        out_specs=VMEM_SPEC,
        scratch_shapes=[
            pltpu.VMEM((slots, LANES), jnp.float32),
            pltpu.VMEM((slots // 3, per_owner * rank), jnp.bfloat16),
        ],
        compiler_params=pltpu.CompilerParams(vmem_limit_bytes=18 * 2**20),
        cost_estimate=COST,
        name="up",
    )(rank_half, recv, adapter_up.reshape(per_owner * rank, hidden), ups, gate_far[1])
    returned = lax.all_to_all(
        offsets.reshape(owners, capacity, hidden), TRUNK, 0, 0, tiled=True
    ).reshape(slots, hidden)
    gates = multiply(gathered, proj_gate, gate_far, flags, offsets)
    gate_parts = lax.all_to_all(after(gates, returned), "x", 0, 0, tiled=True)
    offset = lax.dot_general(
        placed, returned, (((0,), (0,)), ((), ())), preferred_element_type=jnp.float32
    )
    gate_sum = jnp.sum(gate_parts.astype(jnp.float32), axis=0)
    return (jax.nn.silu(gate_sum + offset) * up_sum.astype(jnp.float32)).astype(jnp.bfloat16)


def solution(mesh):
    fine = Mesh(mesh.devices.reshape(2, NX, NZ, 2, 2), TRUNK + ADAPTER)
    placed = (
        P(TRUNK, ADAPTER),
        P(TRUNK),
        P(TRUNK, ADAPTER),
        P(TRUNK, ADAPTER),
        P(TRUNK, ADAPTER, None),
        P(TRUNK, None, ADAPTER),
    )
    return jax.shard_map(
        on_device, mesh=fine, in_specs=placed, out_specs=P(TRUNK, ADAPTER), check_vma=False
    )
```

```python
import functools

import jax
import jax.numpy as jnp
from jax import lax
from jax.experimental import pallas as pl
from jax.experimental.pallas import tpu as pltpu
from jax.sharding import Mesh, PartitionSpec as P

TRUNK = ("yh", "x")
ADAPTER = ("z", "yl", "c")
SWAP = [(0, 1), (1, 0)]
NX, NZ = 4, 8
LANES = 128
HBM_SPEC = pl.BlockSpec(memory_space=pltpu.HBM)
VMEM_SPEC = pl.BlockSpec(memory_space=pltpu.VMEM)
COST = pl.CostEstimate(flops=8 * 10**9, bytes_accessed=16 * 2**20, transcendentals=0)


def after(value, *others):
    return lax.optimization_barrier((value, others))[0]


def start_pairs(flip):
    pairs = []
    for xs in range(NX):
        for h in range(2):
            for xd in range(NX):
                for yl in range(2):
                    source = (xs * NZ + h * NX + xd) * 2 + yl
                    pairs.append((source, (xd * NZ + h * NX + xs) * 2 + (yl ^ flip)))
    return pairs


def multiply_kernel(shifts, flags, rows_ref, own_ref, far_low, far_high, *refs):
    lhs, rhs, lhs_sems, rhs_sems = refs[-4:]
    yh, yl, here = flags[0], flags[1], flags[2]
    count = lhs.shape[0]
    if shifts is None:
        groups, outs = range(count), [refs[-5].at[n] for n in range(count)]
    else:
        groups = [lax.rem(here + shift, NX) for shift in shifts]
        outs = refs[-4 - count : -4]
    depth = own_ref.shape[0]
    width = depth // 4
    weights = []
    for n in range(8):
        block = yh if n < 4 else 1 - yh
        ref = own_ref if n < 4 else (far_low if n < 6 else far_high)
        first = (n % 4 if n < 4 else n % 2) * width
        source_yl, source_core = (n // 2) % 2, n % 2
        y = jnp.where(yl == source_yl, 0, 1)
        to = pl.multiple_of(block * depth + (source_core * 2 + y) * width, width)
        weights.append(
            pltpu.make_async_copy(
                ref.at[pl.ds(first, width), :],
                rhs.at[pl.ds(to, width), :],
                rhs_sems.at[n],
            )
        )
    for copy in weights:
        copy.start()
    rows = [
        [
            pltpu.make_async_copy(
                rows_ref.at[(h * NX + x) * 2 + core],
                lhs.at[n, :, pl.ds((h * 2 + core) * 2 * width, 2 * width)],
                lhs_sems.at[n, h * 2 + core],
            )
            for h in range(2)
            for core in range(2)
        ]
        for n, x in enumerate(groups)
    ]
    for copies in rows:
        for copy in copies:
            copy.start()
    for copy in weights:
        copy.wait()
    for n, copies in enumerate(rows):
        for copy in copies:
            copy.wait()
        outs[n][...] = jnp.dot(
            lhs[n], rhs[...], preferred_element_type=jnp.float32
        ).astype(jnp.bfloat16)


def multiply(rows, weights, weights_far, flags, shifts, *others):
    size = rows.shape[1]
    depth, hidden = weights.shape
    count = NX if shifts is None else len(shifts)
    if shifts is None:
        outs, specs = jax.ShapeDtypeStruct((NX, size, hidden), jnp.bfloat16), VMEM_SPEC
    else:
        outs = [jax.ShapeDtypeStruct((size, hidden), jnp.bfloat16)] * count
        specs = [VMEM_SPEC] * count
    return pl.pallas_call(
        functools.partial(multiply_kernel, shifts),
        out_shape=outs,
        in_specs=[pl.BlockSpec(memory_space=pltpu.SMEM)] + [HBM_SPEC] * (4 + len(others)),
        out_specs=specs,
        scratch_shapes=[
            pltpu.VMEM((count, size, 2 * depth), jnp.bfloat16),
            pltpu.VMEM((2 * depth, hidden), jnp.bfloat16),
            pltpu.SemaphoreType.DMA((count, 4)),
            pltpu.SemaphoreType.DMA((8,)),
        ],
        compiler_params=pltpu.CompilerParams(vmem_limit_bytes=56 * 2**20),
        cost_estimate=COST,
        name="multiply",
    )(flags, rows, weights, *weights_far, *others)


def names_of(recv_ref, tile, rows):
    return recv_ref[pl.ds(tile * rows, rows), 256:].astype(jnp.float32)


def opponent_of(lanes, first, rank):
    return (first + 1 + lax.broadcasted_iota(jnp.int32, (1, lanes), 1) // rank).astype(jnp.float32)


def down_kernel(recv_ref, down_ref, _, out_ref, total):
    slots, rank, width = recv_ref.shape[0], 64, 256
    tiles = 3
    rows = slots // tiles
    total[...] = jnp.zeros_like(total)

    def step(chunk, carry):
        maps = down_ref[pl.ds(pl.multiple_of(chunk * 4 * rank, 4 * rank), 4 * rank), :]
        for tile in range(tiles):
            at = pl.ds(tile * rows, rows)
            product = lax.dot_general(
                recv_ref[at, :width], maps, (((1,), (1,)), ((), ())),
                preferred_element_type=jnp.float32,
            )
            names = names_of(recv_ref, tile, rows)
            first = names == opponent_of(LANES, chunk * 4, rank)
            second = names == opponent_of(LANES, chunk * 4 + 2, rank)
            total[at, :] += jnp.where(first, product[:, :LANES], 0.0) + jnp.where(
                second, product[:, LANES:], 0.0
            )
        return carry

    lax.fori_loop(0, down_ref.shape[0] // (4 * rank), step, 0)
    both = total[...] + pltpu.roll(total[...], rank, 1)
    n = out_ref.shape[0]
    low = both[: 16 * n].reshape(n, 16, LANES)
    high = both[16 * n :].reshape(n, 8, LANES)
    left = lax.broadcasted_iota(jnp.int32, (1, 1, LANES), 2) < rank
    out_ref[:, :8, :] = jnp.where(left, low[:, :8], high)
    out_ref[:, 8:, :] = jnp.where(left, low[:, 8:], 0.0)


def sum_kernel(parts_ref, *refs):
    out_ref = refs[-1]
    total = jnp.sum(parts_ref[...], axis=0).astype(jnp.bfloat16)
    out_ref[...] = jnp.broadcast_to(total[None], out_ref.shape)


def up_kernel(rank_ref, recv_ref, up_ref, *refs):
    out_ref, whole, spread = refs[-3:]
    slots, rank = recv_ref.shape[0], 64
    n = rank_ref.shape[0]
    packed = rank_ref[...].astype(jnp.float32)
    left = lax.broadcasted_iota(jnp.int32, (1, LANES), 1) < rank
    low = packed.reshape(n * 16, LANES)
    high = packed[:, :8].reshape(n * 8, LANES)
    whole[: n * 16, :] = jnp.where(left, low, pltpu.roll(low, rank, 1))
    whole[n * 16 :, :] = jnp.where(left, pltpu.roll(high, rank, 1), high)
    tiles = 3
    rows = slots // tiles

    def step(tile, carry):
        at = pl.ds(pl.multiple_of(tile * rows, rows), rows)
        names = recv_ref[at, 256:].astype(jnp.float32)
        values = whole[at, :]
        for pair in range(up_ref.shape[0] // LANES):
            mine = names == opponent_of(LANES, pair * 2, rank)
            spread[:, pair * LANES : (pair + 1) * LANES] = jnp.where(mine, values, 0.0).astype(
                jnp.bfloat16
            )
        out_ref[at, :] = jnp.dot(
            spread[...], up_ref[...], preferred_element_type=jnp.float32
        ).astype(out_ref.dtype)
        return carry

    lax.fori_loop(0, tiles, step, 0)


def on_device(states, opponent, proj_gate, proj_up, adapter_down, adapter_up):
    rows, width = states.shape
    hidden = proj_gate.shape[1]
    owners = lax.axis_size(TRUNK)
    n_adapter = lax.axis_size(ADAPTER)
    per_owner, _, rank = adapter_down.shape
    capacity = 2 * rows // owners
    slots = owners * capacity
    flags = jnp.stack([lax.axis_index(name) for name in ("yh", "yl", "x")]).astype(jnp.int32)

    mine = lax.ppermute(states, ("x", "z", "yl"), start_pairs(0))
    other = lax.ppermute(states, ("x", "z", "yl"), start_pairs(1))
    cut = proj_up.shape[0] // 2
    up_far, gate_far = (
        [lax.ppermute(part, "yh", SWAP) for part in (weights[:cut], weights[cut:])]
        for weights in (proj_up, proj_gate)
    )

    target = opponent // per_owner
    choose = target[:, None] == jnp.arange(owners, dtype=jnp.int32)[None, :]
    count = jnp.arange(rows, dtype=jnp.int32)
    before = (count[:, None] > count[None, :]).astype(jnp.bfloat16)
    ahead = jnp.dot(before, choose.astype(jnp.bfloat16), preferred_element_type=jnp.float32)
    position = jnp.sum(jnp.where(choose, ahead, 0.0), axis=1).astype(jnp.int32)
    placed = (
        (target * capacity + position)[None, :] == jnp.arange(slots, dtype=jnp.int32)[:, None]
    ).astype(jnp.bfloat16)
    number = jnp.broadcast_to((opponent % per_owner + 1)[:, None], (rows, LANES))
    payload = jnp.concatenate([states, number.astype(jnp.bfloat16)], axis=1)
    send = jnp.dot(placed, payload, preferred_element_type=jnp.float32).astype(jnp.bfloat16)
    recv = lax.all_to_all(
        send.reshape(owners, capacity, width + LANES), TRUNK, 0, 0, tiled=True
    ).reshape(slots, width + LANES)

    mine, other = after((mine, other), send)
    gathered = lax.all_gather(jnp.concatenate([mine, other], axis=1), ("z", "c"), axis=0)

    partial_rank = pl.pallas_call(
        down_kernel,
        out_shape=jax.ShapeDtypeStruct((n_adapter, 16, LANES), jnp.float32),
        in_specs=[VMEM_SPEC] * 2 + [HBM_SPEC],
        out_specs=VMEM_SPEC,
        scratch_shapes=[pltpu.VMEM((slots, LANES), jnp.float32)],
        compiler_params=pltpu.CompilerParams(vmem_limit_bytes=14 * 2**20),
        cost_estimate=COST,
        name="down",
    )(recv, jnp.transpose(adapter_down, (0, 2, 1)).reshape(per_owner * rank, width), up_far[0])
    rank_parts = lax.all_to_all(partial_rank, ADAPTER, 0, 0, tiled=True)
    ups = multiply(gathered, proj_up, up_far, flags, None, partial_rank)
    up_sum = lax.psum_scatter(ups, "x", scatter_dimension=0, tiled=False)
    rank_sum = pl.pallas_call(
        sum_kernel,
        out_shape=jax.ShapeDtypeStruct((n_adapter, 16, LANES), jnp.bfloat16),
        in_specs=[VMEM_SPEC] + [HBM_SPEC] * 2,
        out_specs=VMEM_SPEC,
        cost_estimate=COST,
        name="sum",
    )(rank_parts, ups, gate_far[0])
    rank_half = lax.all_to_all(rank_sum, ADAPTER, 0, 0, tiled=True)

    def send_on(part, shift):
        return lax.ppermute(part, "x", [(i, (i + shift) % NX) for i in range(NX)])

    first = multiply(gathered, proj_gate, gate_far, flags, (2, 1), rank_sum)
    second = multiply(gathered, proj_gate, gate_far, flags, (3, 0), first[0])
    sent = [send_on(first[0], 2), send_on(first[1], 1)]
    gate_parts = sent + [send_on(second[0], 3), second[1]]
    offsets = pl.pallas_call(
        up_kernel,
        out_shape=jax.ShapeDtypeStruct((slots, hidden), jnp.bfloat16),
        in_specs=[VMEM_SPEC] * 3 + [HBM_SPEC] * 3,
        out_specs=VMEM_SPEC,
        scratch_shapes=[
            pltpu.VMEM((slots, LANES), jnp.float32),
            pltpu.VMEM((slots // 3, per_owner * rank), jnp.bfloat16),
        ],
        compiler_params=pltpu.CompilerParams(vmem_limit_bytes=18 * 2**20),
        cost_estimate=COST,
        name="up",
    )(rank_half, recv, adapter_up.reshape(per_owner * rank, hidden), second[1], *sent)
    returned = lax.all_to_all(
        offsets.reshape(owners, capacity, hidden), TRUNK, 0, 0, tiled=True
    ).reshape(slots, hidden)
    offset = lax.dot_general(
        placed, returned, (((0,), (0,)), ((), ())), preferred_element_type=jnp.float32
    )
    gate_sum = functools.reduce(jnp.add, [part.astype(jnp.float32) for part in gate_parts])
    return (jax.nn.silu(gate_sum + offset) * up_sum.astype(jnp.float32)).astype(jnp.bfloat16)


def solution(mesh):
    fine = Mesh(mesh.devices.reshape(2, NX, NZ, 2, 2), TRUNK + ADAPTER)
    placed = (
        P(TRUNK, ADAPTER),
        P(TRUNK),
        P(TRUNK, ADAPTER),
        P(TRUNK, ADAPTER),
        P(TRUNK, ADAPTER, None),
        P(TRUNK, None, ADAPTER),
    )
    return jax.shard_map(
        on_device, mesh=fine, in_specs=placed, out_specs=P(TRUNK, ADAPTER), check_vma=False
    )
```

```python
import functools

import jax
import jax.numpy as jnp
from jax import lax
from jax.experimental import pallas as pl
from jax.experimental.pallas import tpu as pltpu
from jax.sharding import Mesh, PartitionSpec as P

TRUNK = ("yh", "x")
ADAPTER = ("z", "yl", "c")
SWAP = [(0, 1), (1, 0)]
NX, NZ = 4, 8
LANES = 128
NEAR = (0, 1, 2, -1)
HBM_SPEC = pl.BlockSpec(memory_space=pltpu.HBM)
VMEM_SPEC = pl.BlockSpec(memory_space=pltpu.VMEM)
COST = pl.CostEstimate(flops=8 * 10**9, bytes_accessed=16 * 2**20, transcendentals=0)


def after(value, *others):
    return lax.optimization_barrier((value, others))[0]


def start_pairs(flip):
    pairs = []
    for xs in range(NX):
        for h in range(2):
            for xd in range(NX):
                for yl in range(2):
                    z = h * NX + xd
                    to = (z + NEAR[(xs - xd) % NX]) % NZ
                    pairs.append(((xs * NZ + z) * 2 + yl, (xd * NZ + to) * 2 + (yl ^ flip)))
    return pairs


def multiply_kernel(pieces, flags, rows_ref, up_ref, gate_ref, *refs):
    far_refs = refs[: len(pieces)]
    out_ref, done_ref, lhs, rhs, out, lhs_sems, rhs_sems, out_sems = refs[-8:]
    yh, yl, here = flags[0], flags[1], flags[2]
    depth, hidden = up_ref.shape
    width = depth // 4
    chunks = []
    for matrix, ref in enumerate((up_ref, gate_ref)):
        chunks += [(ref, n * width, yh, matrix, n) for n in range(4)]
    for (matrix, first, count), ref in zip(pieces, far_refs):
        chunks += [(ref, n * width, 1 - yh, matrix, first + n) for n in range(count)]
    weights = []
    for n, (ref, at, block, matrix, source) in enumerate(chunks):
        y = jnp.where(yl == source // 2, 0, 1)
        to = pl.multiple_of(block * depth + (source % 2 * 2 + y) * width, width)
        weights.append(
            pltpu.make_async_copy(
                ref.at[pl.ds(at, width), :],
                rhs.at[pl.ds(to, width), pl.ds(matrix * hidden, hidden)],
                rhs_sems.at[n],
            )
        )
    rows, stores = [], []
    for n in range(NX):
        rows.append(
            [
                pltpu.make_async_copy(
                    rows_ref.at[lax.rem(h * NX + here + NEAR[n] + NZ, NZ) * 2 + core],
                    lhs.at[n, :, pl.ds((h * 2 + core) * 2 * width, 2 * width)],
                    lhs_sems.at[n, h * 2 + core],
                )
                for h in range(2)
                for core in range(2)
            ]
        )
        stores.append(
            pltpu.make_async_copy(out.at[n], out_ref.at[lax.rem(here + n, NX)], out_sems.at[n])
        )
    for copy in weights + rows[0] + rows[1]:
        copy.start()
    for copy in weights:
        copy.wait()
    for n in range(NX):
        for copy in rows[n]:
            copy.wait()
        if n + 2 < NX:
            for copy in rows[n + 2]:
                copy.start()
        out[n] = jnp.dot(lhs[n], rhs[...], preferred_element_type=jnp.float32).astype(
            jnp.bfloat16
        )
        stores[n].start()
    done_ref[...] = jnp.zeros_like(done_ref)
    for copy in stores:
        copy.wait()


def multiply(rows, proj_up, proj_gate, far, flags, *others):
    size = rows.shape[1]
    depth, hidden = proj_up.shape
    pieces = [piece[:3] for piece in far]
    return pl.pallas_call(
        functools.partial(multiply_kernel, pieces),
        out_shape=[
            jax.ShapeDtypeStruct((NX, size, 2 * hidden), jnp.bfloat16),
            jax.ShapeDtypeStruct((8, LANES), jnp.float32),
        ],
        in_specs=[pl.BlockSpec(memory_space=pltpu.SMEM)]
        + [HBM_SPEC] * (3 + len(far) + len(others)),
        out_specs=[HBM_SPEC, VMEM_SPEC],
        scratch_shapes=[
            pltpu.VMEM((NX, size, 2 * depth), jnp.bfloat16),
            pltpu.VMEM((2 * depth, 2 * hidden), jnp.bfloat16),
            pltpu.VMEM((NX, size, 2 * hidden), jnp.bfloat16),
            pltpu.SemaphoreType.DMA((NX, 4)),
            pltpu.SemaphoreType.DMA((16,)),
            pltpu.SemaphoreType.DMA((NX,)),
        ],
        compiler_params=pltpu.CompilerParams(vmem_limit_bytes=56 * 2**20),
        cost_estimate=COST,
        name="multiply",
    )(flags, rows, proj_up, proj_gate, *[piece[3] for piece in far], *others)


def names_of(recv_ref, tile, rows):
    return recv_ref[pl.ds(tile * rows, rows), 256:].astype(jnp.float32)


def opponent_of(lanes, first, rank):
    return (first + 1 + lax.broadcasted_iota(jnp.int32, (1, lanes), 1) // rank).astype(jnp.float32)


def down_kernel(recv_ref, down_ref, _, out_ref, total):
    slots, rank, width = recv_ref.shape[0], 64, 256
    tiles = 3
    rows = slots // tiles
    total[...] = jnp.zeros_like(total)

    def step(chunk, carry):
        maps = down_ref[pl.ds(pl.multiple_of(chunk * 4 * rank, 4 * rank), 4 * rank), :]
        for tile in range(tiles):
            at = pl.ds(tile * rows, rows)
            product = lax.dot_general(
                recv_ref[at, :width], maps, (((1,), (1,)), ((), ())),
                preferred_element_type=jnp.float32,
            )
            names = names_of(recv_ref, tile, rows)
            first = names == opponent_of(LANES, chunk * 4, rank)
            second = names == opponent_of(LANES, chunk * 4 + 2, rank)
            total[at, :] += jnp.where(first, product[:, :LANES], 0.0) + jnp.where(
                second, product[:, LANES:], 0.0
            )
        return carry

    lax.fori_loop(0, down_ref.shape[0] // (4 * rank), step, 0)
    both = total[...] + pltpu.roll(total[...], rank, 1)
    n = out_ref.shape[0]
    low = both[: 16 * n].reshape(n, 16, LANES)
    high = both[16 * n :].reshape(n, 8, LANES)
    left = lax.broadcasted_iota(jnp.int32, (1, 1, LANES), 2) < rank
    out_ref[:, :8, :] = jnp.where(left, low[:, :8], high)
    out_ref[:, 8:, :] = jnp.where(left, low[:, 8:], 0.0)


def sum_kernel(parts_ref, *refs):
    out_ref = refs[-1]
    total = jnp.sum(parts_ref[...], axis=0).astype(jnp.bfloat16)
    out_ref[...] = jnp.broadcast_to(total[None], out_ref.shape)


def up_kernel(rank_ref, recv_ref, up_ref, *refs):
    out_ref, whole, spread = refs[-3:]
    slots, rank = recv_ref.shape[0], 64
    n = rank_ref.shape[0]
    packed = rank_ref[...].astype(jnp.float32)
    left = lax.broadcasted_iota(jnp.int32, (1, LANES), 1) < rank
    low = packed.reshape(n * 16, LANES)
    high = packed[:, :8].reshape(n * 8, LANES)
    whole[: n * 16, :] = jnp.where(left, low, pltpu.roll(low, rank, 1))
    whole[n * 16 :, :] = jnp.where(left, pltpu.roll(high, rank, 1), high)
    tiles = 3
    rows = slots // tiles

    def step(tile, carry):
        at = pl.ds(pl.multiple_of(tile * rows, rows), rows)
        names = recv_ref[at, 256:].astype(jnp.float32)
        values = whole[at, :]
        for pair in range(up_ref.shape[0] // LANES):
            mine = names == opponent_of(LANES, pair * 2, rank)
            spread[:, pair * LANES : (pair + 1) * LANES] = jnp.where(mine, values, 0.0).astype(
                jnp.bfloat16
            )
        out_ref[at, :] = jnp.dot(
            spread[...], up_ref[...], preferred_element_type=jnp.float32
        ).astype(out_ref.dtype)
        return carry

    lax.fori_loop(0, tiles, step, 0)


def on_device(states, opponent, proj_gate, proj_up, adapter_down, adapter_up):
    rows, width = states.shape
    hidden = proj_gate.shape[1]
    owners = lax.axis_size(TRUNK)
    n_adapter = lax.axis_size(ADAPTER)
    per_owner, _, rank = adapter_down.shape
    capacity = 2 * rows // owners
    slots = owners * capacity
    flags = jnp.stack([lax.axis_index(name) for name in ("yh", "yl", "x")]).astype(jnp.int32)

    mine = lax.ppermute(states, ("x", "z", "yl"), start_pairs(0))
    other = lax.ppermute(states, ("x", "z", "yl"), start_pairs(1))
    quarter = proj_up.shape[0] // 4

    def swap(matrix, first, count):
        part = (proj_up, proj_gate)[matrix][first * quarter : (first + count) * quarter]
        return matrix, first, count, lax.ppermute(part, "yh", SWAP)

    far = [swap(0, 0, 1), swap(0, 1, 3), swap(1, 0, 2), swap(1, 2, 2)]

    target = opponent // per_owner
    choose = target[:, None] == jnp.arange(owners, dtype=jnp.int32)[None, :]
    count = jnp.arange(rows, dtype=jnp.int32)
    before = (count[:, None] > count[None, :]).astype(jnp.bfloat16)
    ahead = jnp.dot(before, choose.astype(jnp.bfloat16), preferred_element_type=jnp.float32)
    position = jnp.sum(jnp.where(choose, ahead, 0.0), axis=1).astype(jnp.int32)
    placed = (
        (target * capacity + position)[None, :] == jnp.arange(slots, dtype=jnp.int32)[:, None]
    ).astype(jnp.bfloat16)
    number = jnp.broadcast_to((opponent % per_owner + 1)[:, None], (rows, LANES))
    payload = jnp.concatenate([states, number.astype(jnp.bfloat16)], axis=1)
    send = jnp.dot(placed, payload, preferred_element_type=jnp.float32).astype(jnp.bfloat16)
    recv = lax.all_to_all(
        send.reshape(owners, capacity, width + LANES), TRUNK, 0, 0, tiled=True
    ).reshape(slots, width + LANES)

    mine, other = after((mine, other), send, far[0][3])
    gathered = lax.all_gather(jnp.concatenate([mine, other], axis=1), ("z", "c"), axis=0)

    partial_rank = pl.pallas_call(
        down_kernel,
        out_shape=jax.ShapeDtypeStruct((n_adapter, 16, LANES), jnp.float32),
        in_specs=[VMEM_SPEC] * 2 + [HBM_SPEC],
        out_specs=VMEM_SPEC,
        scratch_shapes=[pltpu.VMEM((slots, LANES), jnp.float32)],
        compiler_params=pltpu.CompilerParams(vmem_limit_bytes=14 * 2**20),
        cost_estimate=COST,
        name="down",
    )(recv, jnp.transpose(adapter_down, (0, 2, 1)).reshape(per_owner * rank, width), far[1][3])
    rank_parts = lax.all_to_all(partial_rank, ADAPTER, 0, 0, tiled=True)
    partial, done = multiply(gathered, proj_up, proj_gate, far, flags, rank_parts)
    total = lax.psum_scatter(partial, "x", scatter_dimension=0, tiled=False).astype(jnp.float32)
    rank_sum = pl.pallas_call(
        sum_kernel,
        out_shape=jax.ShapeDtypeStruct((n_adapter, 16, LANES), jnp.bfloat16),
        in_specs=[VMEM_SPEC, HBM_SPEC],
        out_specs=VMEM_SPEC,
        cost_estimate=COST,
        name="sum",
    )(rank_parts, done)
    rank_half = lax.all_to_all(rank_sum, ADAPTER, 0, 0, tiled=True)

    offsets = pl.pallas_call(
        up_kernel,
        out_shape=jax.ShapeDtypeStruct((slots, hidden), jnp.bfloat16),
        in_specs=[VMEM_SPEC] * 3 + [HBM_SPEC],
        out_specs=VMEM_SPEC,
        scratch_shapes=[
            pltpu.VMEM((slots, LANES), jnp.float32),
            pltpu.VMEM((slots // 3, per_owner * rank), jnp.bfloat16),
        ],
        compiler_params=pltpu.CompilerParams(vmem_limit_bytes=18 * 2**20),
        cost_estimate=COST,
        name="up",
    )(rank_half, recv, adapter_up.reshape(per_owner * rank, hidden), done)
    returned = lax.all_to_all(
        offsets.reshape(owners, capacity, hidden), TRUNK, 0, 0, tiled=True
    ).reshape(slots, hidden)
    offset = lax.dot_general(
        placed, returned, (((0,), (0,)), ((), ())), preferred_element_type=jnp.float32
    )
    return (jax.nn.silu(total[:, hidden:] + offset) * total[:, :hidden]).astype(jnp.bfloat16)


def solution(mesh):
    fine = Mesh(mesh.devices.reshape(2, NX, NZ, 2, 2), TRUNK + ADAPTER)
    placed = (
        P(TRUNK, ADAPTER),
        P(TRUNK),
        P(TRUNK, ADAPTER),
        P(TRUNK, ADAPTER),
        P(TRUNK, ADAPTER, None),
        P(TRUNK, None, ADAPTER),
    )
    return jax.shard_map(
        on_device, mesh=fine, in_specs=placed, out_specs=P(TRUNK, ADAPTER), check_vma=False
    )
```

```python
import functools

import jax
import jax.numpy as jnp
from jax import lax
from jax.experimental import pallas as pl
from jax.experimental.pallas import tpu as pltpu
from jax.sharding import Mesh, PartitionSpec as P

TRUNK = ("yh", "x")
ADAPTER = ("z", "yl", "c")
SWAP = [(0, 1), (1, 0)]
NX, NZ = 4, 8
LANES = 128
NEAR = (0, 1, 2, -1)
HBM_SPEC = pl.BlockSpec(memory_space=pltpu.HBM)
VMEM_SPEC = pl.BlockSpec(memory_space=pltpu.VMEM)
COST = pl.CostEstimate(flops=8 * 10**9, bytes_accessed=16 * 2**20, transcendentals=0)


def after(value, *others):
    return lax.optimization_barrier((value, others))[0]


def start_pairs(flip):
    pairs = []
    for xs in range(NX):
        for h in range(2):
            for xd in range(NX):
                for yl in range(2):
                    z = h * NX + xd
                    to = (z + NEAR[(xs - xd) % NX]) % NZ
                    pairs.append(((xs * NZ + z) * 2 + yl, (xd * NZ + to) * 2 + (yl ^ flip)))
    return pairs


def multiply_kernel(pieces, flags, rows_ref, own_ref, *refs):
    far_refs = refs[: len(pieces)]
    out_ref, done_ref, lhs, rhs, out, lhs_sems, rhs_sems, out_sems = refs[-8:]
    yh, yl, here = flags[0], flags[1], flags[2]
    depth = own_ref.shape[0]
    width = depth // 4
    chunks = [(own_ref, n * width, yh, n) for n in range(4)]
    for (first, count), ref in zip(pieces, far_refs):
        chunks += [(ref, n * width, 1 - yh, first + n) for n in range(count)]
    weights = []
    for n, (ref, at, block, source) in enumerate(chunks):
        y = jnp.where(yl == source // 2, 0, 1)
        to = pl.multiple_of(block * depth + (source % 2 * 2 + y) * width, width)
        weights.append(
            pltpu.make_async_copy(
                ref.at[pl.ds(at, width), :], rhs.at[pl.ds(to, width), :], rhs_sems.at[n]
            )
        )
    rows, stores = [], []
    for n in range(NX):
        rows.append(
            [
                pltpu.make_async_copy(
                    rows_ref.at[lax.rem(h * NX + here + NEAR[n] + NZ, NZ) * 2 + core],
                    lhs.at[n, :, pl.ds((h * 2 + core) * 2 * width, 2 * width)],
                    lhs_sems.at[n, h * 2 + core],
                )
                for h in range(2)
                for core in range(2)
            ]
        )
        stores.append(
            pltpu.make_async_copy(out.at[n], out_ref.at[lax.rem(here + n, NX)], out_sems.at[n])
        )
    for copy in weights + rows[0]:
        copy.start()
    for copy in weights:
        copy.wait()
    for n in range(NX):
        for copy in rows[n]:
            copy.wait()
        if n + 1 < NX:
            for copy in rows[n + 1]:
                copy.start()
        out[n] = jnp.dot(lhs[n], rhs[...], preferred_element_type=jnp.float32).astype(
            jnp.bfloat16
        )
        stores[n].start()
    done_ref[...] = jnp.zeros_like(done_ref)
    for copy in stores:
        copy.wait()


def multiply(rows, weights, far, flags, *others):
    size = rows.shape[1]
    depth, hidden = weights.shape
    pieces = [piece[:2] for piece in far]
    return pl.pallas_call(
        functools.partial(multiply_kernel, pieces),
        out_shape=[
            jax.ShapeDtypeStruct((NX, size, hidden), jnp.bfloat16),
            jax.ShapeDtypeStruct((8, LANES), jnp.float32),
        ],
        in_specs=[pl.BlockSpec(memory_space=pltpu.SMEM)]
        + [HBM_SPEC] * (2 + len(far) + len(others)),
        out_specs=[HBM_SPEC, VMEM_SPEC],
        scratch_shapes=[
            pltpu.VMEM((NX, size, 2 * depth), jnp.bfloat16),
            pltpu.VMEM((2 * depth, hidden), jnp.bfloat16),
            pltpu.VMEM((NX, size, hidden), jnp.bfloat16),
            pltpu.SemaphoreType.DMA((NX, 4)),
            pltpu.SemaphoreType.DMA((8,)),
            pltpu.SemaphoreType.DMA((NX,)),
        ],
        compiler_params=pltpu.CompilerParams(vmem_limit_bytes=56 * 2**20),
        cost_estimate=COST,
        name="multiply",
    )(flags, rows, weights, *[piece[2] for piece in far], *others)


def names_of(recv_ref, tile, rows):
    return recv_ref[pl.ds(tile * rows, rows), 256:].astype(jnp.float32)


def opponent_of(lanes, first, rank):
    return (first + 1 + lax.broadcasted_iota(jnp.int32, (1, lanes), 1) // rank).astype(jnp.float32)


def down_kernel(recv_ref, down_ref, _, out_ref, total):
    slots, rank, width = recv_ref.shape[0], 64, 256
    tiles = 3
    rows = slots // tiles
    total[...] = jnp.zeros_like(total)

    def step(chunk, carry):
        maps = down_ref[pl.ds(pl.multiple_of(chunk * 4 * rank, 4 * rank), 4 * rank), :]
        for tile in range(tiles):
            at = pl.ds(tile * rows, rows)
            product = lax.dot_general(
                recv_ref[at, :width], maps, (((1,), (1,)), ((), ())),
                preferred_element_type=jnp.float32,
            )
            names = names_of(recv_ref, tile, rows)
            first = names == opponent_of(LANES, chunk * 4, rank)
            second = names == opponent_of(LANES, chunk * 4 + 2, rank)
            total[at, :] += jnp.where(first, product[:, :LANES], 0.0) + jnp.where(
                second, product[:, LANES:], 0.0
            )
        return carry

    lax.fori_loop(0, down_ref.shape[0] // (4 * rank), step, 0)
    both = total[...] + pltpu.roll(total[...], rank, 1)
    n = out_ref.shape[0]
    low = both[: 16 * n].reshape(n, 16, LANES)
    high = both[16 * n :].reshape(n, 8, LANES)
    left = lax.broadcasted_iota(jnp.int32, (1, 1, LANES), 2) < rank
    out_ref[:, :8, :] = jnp.where(left, low[:, :8], high)
    out_ref[:, 8:, :] = jnp.where(left, low[:, 8:], 0.0)


def sum_kernel(parts_ref, *refs):
    out_ref = refs[-1]
    total = jnp.sum(parts_ref[...], axis=0).astype(jnp.bfloat16)
    out_ref[...] = jnp.broadcast_to(total[None], out_ref.shape)


def up_kernel(rank_ref, recv_ref, up_ref, *refs):
    out_ref, whole, spread = refs[-3:]
    slots, rank = recv_ref.shape[0], 64
    n = rank_ref.shape[0]
    packed = rank_ref[...].astype(jnp.float32)
    left = lax.broadcasted_iota(jnp.int32, (1, LANES), 1) < rank
    low = packed.reshape(n * 16, LANES)
    high = packed[:, :8].reshape(n * 8, LANES)
    whole[: n * 16, :] = jnp.where(left, low, pltpu.roll(low, rank, 1))
    whole[n * 16 :, :] = jnp.where(left, pltpu.roll(high, rank, 1), high)
    tiles = 3
    rows = slots // tiles

    def step(tile, carry):
        at = pl.ds(pl.multiple_of(tile * rows, rows), rows)
        names = recv_ref[at, 256:].astype(jnp.float32)
        values = whole[at, :]
        for pair in range(up_ref.shape[0] // LANES):
            mine = names == opponent_of(LANES, pair * 2, rank)
            spread[:, pair * LANES : (pair + 1) * LANES] = jnp.where(mine, values, 0.0).astype(
                jnp.bfloat16
            )
        out_ref[at, :] = jnp.dot(
            spread[...], up_ref[...], preferred_element_type=jnp.float32
        ).astype(out_ref.dtype)
        return carry

    lax.fori_loop(0, tiles, step, 0)


def on_device(states, opponent, proj_gate, proj_up, adapter_down, adapter_up):
    rows, width = states.shape
    hidden = proj_gate.shape[1]
    owners = lax.axis_size(TRUNK)
    n_adapter = lax.axis_size(ADAPTER)
    per_owner, _, rank = adapter_down.shape
    capacity = 2 * rows // owners
    slots = owners * capacity
    flags = jnp.stack([lax.axis_index(name) for name in ("yh", "yl", "x")]).astype(jnp.int32)

    mine = lax.ppermute(states, ("x", "z", "yl"), start_pairs(0))
    other = lax.ppermute(states, ("x", "z", "yl"), start_pairs(1))
    quarter = proj_up.shape[0] // 4

    def swap(weights, first, count, *others):
        part = weights[first * quarter : (first + count) * quarter]
        return first, count, lax.ppermute(after(part, *others), "yh", SWAP)

    up_far = [swap(proj_up, 0, 1), swap(proj_up, 1, 3)]

    target = opponent // per_owner
    choose = target[:, None] == jnp.arange(owners, dtype=jnp.int32)[None, :]
    count = jnp.arange(rows, dtype=jnp.int32)
    before = (count[:, None] > count[None, :]).astype(jnp.bfloat16)
    ahead = jnp.dot(before, choose.astype(jnp.bfloat16), preferred_element_type=jnp.float32)
    position = jnp.sum(jnp.where(choose, ahead, 0.0), axis=1).astype(jnp.int32)
    placed = (
        (target * capacity + position)[None, :] == jnp.arange(slots, dtype=jnp.int32)[:, None]
    ).astype(jnp.bfloat16)
    number = jnp.broadcast_to((opponent % per_owner + 1)[:, None], (rows, LANES))
    payload = jnp.concatenate([states, number.astype(jnp.bfloat16)], axis=1)
    send = jnp.dot(placed, payload, preferred_element_type=jnp.float32).astype(jnp.bfloat16)
    recv = lax.all_to_all(
        send.reshape(owners, capacity, width + LANES), TRUNK, 0, 0, tiled=True
    ).reshape(slots, width + LANES)

    mine, other = after((mine, other), send, up_far[0][2])
    gathered = lax.all_gather(jnp.concatenate([mine, other], axis=1), ("z", "c"), axis=0)

    gate_far = [swap(proj_gate, 0, 2, recv), swap(proj_gate, 2, 2, recv)]
    partial_rank = pl.pallas_call(
        down_kernel,
        out_shape=jax.ShapeDtypeStruct((n_adapter, 16, LANES), jnp.float32),
        in_specs=[VMEM_SPEC] * 2 + [HBM_SPEC],
        out_specs=VMEM_SPEC,
        scratch_shapes=[pltpu.VMEM((slots, LANES), jnp.float32)],
        compiler_params=pltpu.CompilerParams(vmem_limit_bytes=14 * 2**20),
        cost_estimate=COST,
        name="down",
    )(recv, jnp.transpose(adapter_down, (0, 2, 1)).reshape(per_owner * rank, width), up_far[1][2])
    rank_parts = lax.all_to_all(partial_rank, ADAPTER, 0, 0, tiled=True)
    def finish(partial):
        return lax.psum_scatter(partial, "x", scatter_dimension=0, tiled=False).astype(jnp.float32)

    ups, done = multiply(gathered, proj_up, up_far, flags, rank_parts, gate_far[0][2])
    up_sum = finish(ups)
    rank_sum = pl.pallas_call(
        sum_kernel,
        out_shape=jax.ShapeDtypeStruct((n_adapter, 16, LANES), jnp.bfloat16),
        in_specs=[VMEM_SPEC] + [HBM_SPEC],
        out_specs=VMEM_SPEC,
        cost_estimate=COST,
        name="sum",
    )(rank_parts, done)
    rank_half = lax.all_to_all(rank_sum, ADAPTER, 0, 0, tiled=True)
    gates, done = multiply(gathered, proj_gate, gate_far, flags, rank_half)
    gate_sum = finish(gates)

    offsets = pl.pallas_call(
        up_kernel,
        out_shape=jax.ShapeDtypeStruct((slots, hidden), jnp.bfloat16),
        in_specs=[VMEM_SPEC] * 3 + [HBM_SPEC],
        out_specs=VMEM_SPEC,
        scratch_shapes=[
            pltpu.VMEM((slots, LANES), jnp.float32),
            pltpu.VMEM((slots // 3, per_owner * rank), jnp.bfloat16),
        ],
        compiler_params=pltpu.CompilerParams(vmem_limit_bytes=18 * 2**20),
        cost_estimate=COST,
        name="up",
    )(rank_half, recv, adapter_up.reshape(per_owner * rank, hidden), done)
    returned = lax.all_to_all(
        offsets.reshape(owners, capacity, hidden), TRUNK, 0, 0, tiled=True
    ).reshape(slots, hidden)
    offset = lax.dot_general(
        placed, returned, (((0,), (0,)), ((), ())), preferred_element_type=jnp.float32
    )
    return (jax.nn.silu(gate_sum + offset) * up_sum).astype(jnp.bfloat16)


def solution(mesh):
    fine = Mesh(mesh.devices.reshape(2, NX, NZ, 2, 2), TRUNK + ADAPTER)
    placed = (
        P(TRUNK, ADAPTER),
        P(TRUNK),
        P(TRUNK, ADAPTER),
        P(TRUNK, ADAPTER),
        P(TRUNK, ADAPTER, None),
        P(TRUNK, None, ADAPTER),
    )
    return jax.shard_map(
        on_device, mesh=fine, in_specs=placed, out_specs=P(TRUNK, ADAPTER), check_vma=False
    )
```

```python
import functools

import jax
import jax.numpy as jnp
from jax import lax
from jax.experimental import pallas as pl
from jax.experimental.pallas import tpu as pltpu
from jax.sharding import Mesh, PartitionSpec as P

TRUNK = ("yh", "x")
ADAPTER = ("z", "yl", "c")
SWAP = [(0, 1), (1, 0)]
NX, NZ = 4, 8
LANES = 128
NEAR = (0, 1, 2, -1)
HBM_SPEC = pl.BlockSpec(memory_space=pltpu.HBM)
VMEM_SPEC = pl.BlockSpec(memory_space=pltpu.VMEM)
COST = pl.CostEstimate(flops=8 * 10**9, bytes_accessed=16 * 2**20, transcendentals=0)


def after(value, *others):
    return lax.optimization_barrier((value, others))[0]


def start_pairs(flip):
    pairs = []
    for xs in range(NX):
        for h in range(2):
            for xd in range(NX):
                for yl in range(2):
                    z = h * NX + xd
                    to = (z + NEAR[(xs - xd) % NX]) % NZ
                    pairs.append(((xs * NZ + z) * 2 + yl, (xd * NZ + to) * 2 + (yl ^ flip)))
    return pairs


def multiply_kernel(pieces, flags, rows_ref, own_ref, *refs):
    far_refs = refs[: len(pieces)]
    out_ref, done_ref, lhs, rhs, out, lhs_sems, rhs_sems, out_sems = refs[-8:]
    yh, yl, here = flags[0], flags[1], flags[2]
    depth = own_ref.shape[0]
    width = depth // 4
    chunks = [(own_ref, n * width, yh, n) for n in range(4)]
    for (first, count), ref in zip(pieces, far_refs):
        chunks += [(ref, n * width, 1 - yh, first + n) for n in range(count)]
    weights = []
    for n, (ref, at, block, source) in enumerate(chunks):
        y = jnp.where(yl == source // 2, 0, 1)
        to = pl.multiple_of(block * depth + (source % 2 * 2 + y) * width, width)
        weights.append(
            pltpu.make_async_copy(
                ref.at[pl.ds(at, width), :], rhs.at[pl.ds(to, width), :], rhs_sems.at[n]
            )
        )
    rows, stores = [], []
    for n in range(NX):
        rows.append(
            [
                pltpu.make_async_copy(
                    rows_ref.at[lax.rem(h * NX + here + NEAR[n] + NZ, NZ) * 2 + core],
                    lhs.at[n, :, pl.ds((h * 2 + core) * 2 * width, 2 * width)],
                    lhs_sems.at[n, h * 2 + core],
                )
                for h in range(2)
                for core in range(2)
            ]
        )
        stores.append(
            pltpu.make_async_copy(out.at[n], out_ref.at[lax.rem(here + n, NX)], out_sems.at[n])
        )
    for copy in weights + rows[0]:
        copy.start()
    for copy in weights:
        copy.wait()
    for n in range(NX):
        for copy in rows[n]:
            copy.wait()
        if n + 1 < NX:
            for copy in rows[n + 1]:
                copy.start()
        out[n] = jnp.dot(lhs[n], rhs[...], preferred_element_type=jnp.float32).astype(
            jnp.bfloat16
        )
        stores[n].start()
    done_ref[...] = jnp.zeros_like(done_ref)
    for copy in stores:
        copy.wait()


def multiply(rows, weights, far, flags, *others):
    size = rows.shape[1]
    depth, hidden = weights.shape
    pieces = [piece[:2] for piece in far]
    return pl.pallas_call(
        functools.partial(multiply_kernel, pieces),
        out_shape=[
            jax.ShapeDtypeStruct((NX, size, hidden), jnp.bfloat16),
            jax.ShapeDtypeStruct((8, LANES), jnp.float32),
        ],
        in_specs=[pl.BlockSpec(memory_space=pltpu.SMEM)]
        + [HBM_SPEC] * (2 + len(far) + len(others)),
        out_specs=[HBM_SPEC, VMEM_SPEC],
        scratch_shapes=[
            pltpu.VMEM((NX, size, 2 * depth), jnp.bfloat16),
            pltpu.VMEM((2 * depth, hidden), jnp.bfloat16),
            pltpu.VMEM((NX, size, hidden), jnp.bfloat16),
            pltpu.SemaphoreType.DMA((NX, 4)),
            pltpu.SemaphoreType.DMA((8,)),
            pltpu.SemaphoreType.DMA((NX,)),
        ],
        compiler_params=pltpu.CompilerParams(vmem_limit_bytes=56 * 2**20),
        cost_estimate=COST,
        name="multiply",
    )(flags, rows, weights, *[piece[2] for piece in far], *others)


def names_of(recv_ref, tile, rows):
    return recv_ref[pl.ds(tile * rows, rows), 256:].astype(jnp.float32)


def opponent_of(lanes, first, rank):
    return (first + 1 + lax.broadcasted_iota(jnp.int32, (1, lanes), 1) // rank).astype(jnp.float32)


def down_kernel(recv_ref, down_ref, out_ref, total):
    slots, rank, width = recv_ref.shape[0], 64, 256
    tiles = 3
    rows = slots // tiles
    total[...] = jnp.zeros_like(total)

    def step(chunk, carry):
        maps = down_ref[pl.ds(pl.multiple_of(chunk * 4 * rank, 4 * rank), 4 * rank), :]
        for tile in range(tiles):
            at = pl.ds(tile * rows, rows)
            product = lax.dot_general(
                recv_ref[at, :width], maps, (((1,), (1,)), ((), ())),
                preferred_element_type=jnp.float32,
            )
            names = names_of(recv_ref, tile, rows)
            first = names == opponent_of(LANES, chunk * 4, rank)
            second = names == opponent_of(LANES, chunk * 4 + 2, rank)
            total[at, :] += jnp.where(first, product[:, :LANES], 0.0) + jnp.where(
                second, product[:, LANES:], 0.0
            )
        return carry

    lax.fori_loop(0, down_ref.shape[0] // (4 * rank), step, 0)
    both = total[...] + pltpu.roll(total[...], rank, 1)
    n = out_ref.shape[0]
    low = both[: 16 * n].reshape(n, 16, LANES)
    high = both[16 * n :].reshape(n, 8, LANES)
    left = lax.broadcasted_iota(jnp.int32, (1, 1, LANES), 2) < rank
    out_ref[:, :8, :] = jnp.where(left, low[:, :8], high)
    out_ref[:, 8:, :] = jnp.where(left, low[:, 8:], 0.0)


def sum_kernel(parts_ref, *refs):
    out_ref = refs[-1]
    total = jnp.sum(parts_ref[...], axis=0).astype(jnp.bfloat16)
    out_ref[...] = jnp.broadcast_to(total[None], out_ref.shape)


def up_kernel(rank_ref, recv_ref, up_ref, *refs):
    out_ref, whole, spread = refs[-3:]
    slots, rank = recv_ref.shape[0], 64
    n = rank_ref.shape[0]
    packed = rank_ref[...].astype(jnp.float32)
    left = lax.broadcasted_iota(jnp.int32, (1, LANES), 1) < rank
    low = packed.reshape(n * 16, LANES)
    high = packed[:, :8].reshape(n * 8, LANES)
    whole[: n * 16, :] = jnp.where(left, low, pltpu.roll(low, rank, 1))
    whole[n * 16 :, :] = jnp.where(left, pltpu.roll(high, rank, 1), high)
    tiles = 3
    rows = slots // tiles

    def step(tile, carry):
        at = pl.ds(pl.multiple_of(tile * rows, rows), rows)
        names = recv_ref[at, 256:].astype(jnp.float32)
        values = whole[at, :]
        for pair in range(up_ref.shape[0] // LANES):
            mine = names == opponent_of(LANES, pair * 2, rank)
            spread[:, pair * LANES : (pair + 1) * LANES] = jnp.where(mine, values, 0.0).astype(
                jnp.bfloat16
            )
        out_ref[at, :] = jnp.dot(
            spread[...], up_ref[...], preferred_element_type=jnp.float32
        ).astype(out_ref.dtype)
        return carry

    lax.fori_loop(0, tiles, step, 0)


def on_device(states, opponent, proj_gate, proj_up, adapter_down, adapter_up):
    rows, width = states.shape
    hidden = proj_gate.shape[1]
    owners = lax.axis_size(TRUNK)
    n_adapter = lax.axis_size(ADAPTER)
    per_owner, _, rank = adapter_down.shape
    capacity = 2 * rows // owners
    slots = owners * capacity
    flags = jnp.stack([lax.axis_index(name) for name in ("yh", "yl", "x")]).astype(jnp.int32)

    mine = lax.ppermute(states, ("x", "z", "yl"), start_pairs(0))
    other = lax.ppermute(states, ("x", "z", "yl"), start_pairs(1))
    quarter = proj_up.shape[0] // 4

    def swap(weights, first, count, *others):
        part = weights[first * quarter : (first + count) * quarter]
        return first, count, lax.ppermute(after(part, *others), "yh", SWAP)

    up_far = [swap(proj_up, 0, 1)]

    target = opponent // per_owner
    choose = target[:, None] == jnp.arange(owners, dtype=jnp.int32)[None, :]
    count = jnp.arange(rows, dtype=jnp.int32)
    before = (count[:, None] > count[None, :]).astype(jnp.bfloat16)
    ahead = jnp.dot(before, choose.astype(jnp.bfloat16), preferred_element_type=jnp.float32)
    position = jnp.sum(jnp.where(choose, ahead, 0.0), axis=1).astype(jnp.int32)
    placed = (
        (target * capacity + position)[None, :] == jnp.arange(slots, dtype=jnp.int32)[:, None]
    ).astype(jnp.bfloat16)
    number = jnp.broadcast_to((opponent % per_owner + 1)[:, None], (rows, LANES))
    payload = jnp.concatenate([states, number.astype(jnp.bfloat16)], axis=1)
    send = jnp.dot(placed, payload, preferred_element_type=jnp.float32).astype(jnp.bfloat16)
    recv = lax.all_to_all(
        send.reshape(owners, capacity, width + LANES), TRUNK, 0, 0, tiled=True
    ).reshape(slots, width + LANES)

    mine, other = after((mine, other), send, up_far[0][2])
    gathered = lax.all_gather(jnp.concatenate([mine, other], axis=1), ("z", "c"), axis=0)

    up_far.append(swap(proj_up, 1, 3, recv))
    partial_rank = pl.pallas_call(
        down_kernel,
        out_shape=jax.ShapeDtypeStruct((n_adapter, 16, LANES), jnp.float32),
        in_specs=[VMEM_SPEC] * 2,
        out_specs=VMEM_SPEC,
        scratch_shapes=[pltpu.VMEM((slots, LANES), jnp.float32)],
        compiler_params=pltpu.CompilerParams(vmem_limit_bytes=14 * 2**20),
        cost_estimate=COST,
        name="down",
    )(recv, jnp.transpose(adapter_down, (0, 2, 1)).reshape(per_owner * rank, width))
    rank_parts = lax.all_to_all(partial_rank, ADAPTER, 0, 0, tiled=True)
    rank_sum = pl.pallas_call(
        sum_kernel,
        out_shape=jax.ShapeDtypeStruct((n_adapter, 16, LANES), jnp.bfloat16),
        in_specs=[VMEM_SPEC, HBM_SPEC],
        out_specs=VMEM_SPEC,
        cost_estimate=COST,
        name="sum",
    )(rank_parts, up_far[1][2])
    rank_half = lax.all_to_all(rank_sum, ADAPTER, 0, 0, tiled=True)
    gate_far = [swap(proj_gate, first, 2, rank_sum) for first in (0, 2)]

    def finish(partial):
        return lax.psum_scatter(partial, "x", scatter_dimension=0, tiled=False).astype(jnp.float32)

    ups, done = multiply(gathered, proj_up, up_far, flags, rank_half, gate_far[0][2])
    up_sum = finish(ups)
    offsets = pl.pallas_call(
        up_kernel,
        out_shape=jax.ShapeDtypeStruct((slots, hidden), jnp.bfloat16),
        in_specs=[VMEM_SPEC] * 3 + [HBM_SPEC],
        out_specs=VMEM_SPEC,
        scratch_shapes=[
            pltpu.VMEM((slots, LANES), jnp.float32),
            pltpu.VMEM((slots // 3, per_owner * rank), jnp.bfloat16),
        ],
        compiler_params=pltpu.CompilerParams(vmem_limit_bytes=18 * 2**20),
        cost_estimate=COST,
        name="up",
    )(rank_half, recv, adapter_up.reshape(per_owner * rank, hidden), done)
    returned = lax.all_to_all(
        offsets.reshape(owners, capacity, hidden), TRUNK, 0, 0, tiled=True
    ).reshape(slots, hidden)
    gates, _ = multiply(gathered, proj_gate, gate_far, flags, offsets)
    gate_sum = finish(gates)
    offset = lax.dot_general(
        placed, returned, (((0,), (0,)), ((), ())), preferred_element_type=jnp.float32
    )
    return (jax.nn.silu(gate_sum + offset) * up_sum).astype(jnp.bfloat16)


def solution(mesh):
    fine = Mesh(mesh.devices.reshape(2, NX, NZ, 2, 2), TRUNK + ADAPTER)
    placed = (
        P(TRUNK, ADAPTER),
        P(TRUNK),
        P(TRUNK, ADAPTER),
        P(TRUNK, ADAPTER),
        P(TRUNK, ADAPTER, None),
        P(TRUNK, None, ADAPTER),
    )
    return jax.shard_map(
        on_device, mesh=fine, in_specs=placed, out_specs=P(TRUNK, ADAPTER), check_vma=False
    )
```

```python
import functools

import jax
import jax.numpy as jnp
from jax import lax
from jax.experimental import pallas as pl
from jax.experimental.pallas import tpu as pltpu
from jax.sharding import Mesh, PartitionSpec as P

TRUNK = ("yh", "x")
ADAPTER = ("z", "yl", "c")
SWAP = [(0, 1), (1, 0)]
NX, NZ = 4, 8
LANES = 128
NEAR = (0, 1, 2, -1)
HBM_SPEC = pl.BlockSpec(memory_space=pltpu.HBM)
VMEM_SPEC = pl.BlockSpec(memory_space=pltpu.VMEM)
COST = pl.CostEstimate(flops=8 * 10**9, bytes_accessed=16 * 2**20, transcendentals=0)


def after(value, *others):
    return lax.optimization_barrier((value, others))[0]


def start_pairs(flip):
    pairs = []
    for xs in range(NX):
        for h in range(2):
            for xd in range(NX):
                for yl in range(2):
                    z = h * NX + xd
                    to = (z + NEAR[(xs - xd) % NX]) % NZ
                    pairs.append(((xs * NZ + z) * 2 + yl, (xd * NZ + to) * 2 + (yl ^ flip)))
    return pairs


def multiply_kernel(pieces, flags, rows_ref, own_ref, *refs):
    far_refs = refs[: len(pieces)]
    out_ref, done_ref, lhs, rhs, out, lhs_sems, rhs_sems, out_sems = refs[-8:]
    yh, yl, here = flags[0], flags[1], flags[2]
    depth = own_ref.shape[0]
    width = depth // 4
    chunks = [(own_ref, n * width, yh, n) for n in range(4)]
    for (first, count), ref in zip(pieces, far_refs):
        chunks += [(ref, n * width, 1 - yh, first + n) for n in range(count)]
    weights = []
    for n, (ref, at, block, source) in enumerate(chunks):
        y = jnp.where(yl == source // 2, 0, 1)
        to = pl.multiple_of(block * depth + (source % 2 * 2 + y) * width, width)
        weights.append(
            pltpu.make_async_copy(
                ref.at[pl.ds(at, width), :], rhs.at[pl.ds(to, width), :], rhs_sems.at[n]
            )
        )
    rows, stores = [], []
    for n in range(NX):
        rows.append(
            [
                pltpu.make_async_copy(
                    rows_ref.at[lax.rem(h * NX + here + NEAR[n] + NZ, NZ) * 2 + core],
                    lhs.at[n, :, pl.ds((h * 2 + core) * 2 * width, 2 * width)],
                    lhs_sems.at[n, h * 2 + core],
                )
                for h in range(2)
                for core in range(2)
            ]
        )
        stores.append(
            pltpu.make_async_copy(out.at[n], out_ref.at[lax.rem(here + n, NX)], out_sems.at[n])
        )
    for copy in weights + rows[0]:
        copy.start()
    for copy in weights:
        copy.wait()
    for n in range(NX):
        for copy in rows[n]:
            copy.wait()
        if n + 1 < NX:
            for copy in rows[n + 1]:
                copy.start()
        out[n] = jnp.dot(lhs[n], rhs[...], preferred_element_type=jnp.float32).astype(
            jnp.bfloat16
        )
        stores[n].start()
    done_ref[...] = jnp.zeros_like(done_ref)
    for copy in stores:
        copy.wait()


def multiply(rows, weights, far, flags, *others):
    size = rows.shape[1]
    depth, hidden = weights.shape
    pieces = [piece[:2] for piece in far]
    return pl.pallas_call(
        functools.partial(multiply_kernel, pieces),
        out_shape=[
            jax.ShapeDtypeStruct((NX, size, hidden), jnp.bfloat16),
            jax.ShapeDtypeStruct((8, LANES), jnp.float32),
        ],
        in_specs=[pl.BlockSpec(memory_space=pltpu.SMEM)]
        + [HBM_SPEC] * (2 + len(far) + len(others)),
        out_specs=[HBM_SPEC, VMEM_SPEC],
        scratch_shapes=[
            pltpu.VMEM((NX, size, 2 * depth), jnp.bfloat16),
            pltpu.VMEM((2 * depth, hidden), jnp.bfloat16),
            pltpu.VMEM((NX, size, hidden), jnp.bfloat16),
            pltpu.SemaphoreType.DMA((NX, 4)),
            pltpu.SemaphoreType.DMA((8,)),
            pltpu.SemaphoreType.DMA((NX,)),
        ],
        compiler_params=pltpu.CompilerParams(vmem_limit_bytes=56 * 2**20),
        cost_estimate=COST,
        name="multiply",
    )(flags, rows, weights, *[piece[2] for piece in far], *others)


def names_of(recv_ref, tile, rows):
    return recv_ref[pl.ds(tile * rows, rows), 256:].astype(jnp.float32)


def opponent_of(lanes, first, rank):
    return (first + 1 + lax.broadcasted_iota(jnp.int32, (1, lanes), 1) // rank).astype(jnp.float32)


def down_kernel(recv_ref, down_ref, out_ref, total):
    slots, rank, width = recv_ref.shape[0], 64, 256
    tiles = 3
    rows = slots // tiles
    total[...] = jnp.zeros_like(total)

    def step(chunk, carry):
        maps = down_ref[pl.ds(pl.multiple_of(chunk * 4 * rank, 4 * rank), 4 * rank), :]
        for tile in range(tiles):
            at = pl.ds(tile * rows, rows)
            product = lax.dot_general(
                recv_ref[at, :width], maps, (((1,), (1,)), ((), ())),
                preferred_element_type=jnp.float32,
            )
            names = names_of(recv_ref, tile, rows)
            first = names == opponent_of(LANES, chunk * 4, rank)
            second = names == opponent_of(LANES, chunk * 4 + 2, rank)
            total[at, :] += jnp.where(first, product[:, :LANES], 0.0) + jnp.where(
                second, product[:, LANES:], 0.0
            )
        return carry

    lax.fori_loop(0, down_ref.shape[0] // (4 * rank), step, 0)
    both = total[...] + pltpu.roll(total[...], rank, 1)
    n = out_ref.shape[0]
    low = both[: 16 * n].reshape(n, 16, LANES)
    high = both[16 * n :].reshape(n, 8, LANES)
    left = lax.broadcasted_iota(jnp.int32, (1, 1, LANES), 2) < rank
    out_ref[:, :8, :] = jnp.where(left, low[:, :8], high)
    out_ref[:, 8:, :] = jnp.where(left, low[:, 8:], 0.0)


def sum_kernel(parts_ref, *refs):
    out_ref = refs[-1]
    total = jnp.sum(parts_ref[...], axis=0).astype(jnp.bfloat16)
    out_ref[...] = jnp.broadcast_to(total[None], out_ref.shape)


def up_kernel(rank_ref, recv_ref, up_ref, *refs):
    out_ref, whole, spread = refs[-3:]
    slots, rank = recv_ref.shape[0], 64
    n = rank_ref.shape[0]
    packed = rank_ref[...].astype(jnp.float32)
    left = lax.broadcasted_iota(jnp.int32, (1, LANES), 1) < rank
    low = packed.reshape(n * 16, LANES)
    high = packed[:, :8].reshape(n * 8, LANES)
    whole[: n * 16, :] = jnp.where(left, low, pltpu.roll(low, rank, 1))
    whole[n * 16 :, :] = jnp.where(left, pltpu.roll(high, rank, 1), high)
    tiles = 3
    rows = slots // tiles

    def step(tile, carry):
        at = pl.ds(pl.multiple_of(tile * rows, rows), rows)
        names = recv_ref[at, 256:].astype(jnp.float32)
        values = whole[at, :]
        for pair in range(up_ref.shape[0] // LANES):
            mine = names == opponent_of(LANES, pair * 2, rank)
            spread[:, pair * LANES : (pair + 1) * LANES] = jnp.where(mine, values, 0.0).astype(
                jnp.bfloat16
            )
        out_ref[at, :] = jnp.dot(
            spread[...], up_ref[...], preferred_element_type=jnp.float32
        ).astype(out_ref.dtype)
        return carry

    lax.fori_loop(0, tiles, step, 0)


def on_device(states, opponent, proj_gate, proj_up, adapter_down, adapter_up):
    rows, width = states.shape
    hidden = proj_gate.shape[1]
    owners = lax.axis_size(TRUNK)
    n_adapter = lax.axis_size(ADAPTER)
    per_owner, _, rank = adapter_down.shape
    capacity = 2 * rows // owners
    slots = owners * capacity
    flags = jnp.stack([lax.axis_index(name) for name in ("yh", "yl", "x")]).astype(jnp.int32)

    mine = lax.ppermute(states, ("x", "z", "yl"), start_pairs(0))
    other = lax.ppermute(states, ("x", "z", "yl"), start_pairs(1))
    quarter = proj_up.shape[0] // 4

    def swap(weights, first, count, *others):
        part = weights[first * quarter : (first + count) * quarter]
        return first, count, lax.ppermute(after(part, *others), "yh", SWAP)

    up_far = [swap(proj_up, 0, 1)]

    target = opponent // per_owner
    choose = target[:, None] == jnp.arange(owners, dtype=jnp.int32)[None, :]
    count = jnp.arange(rows, dtype=jnp.int32)
    before = (count[:, None] > count[None, :]).astype(jnp.bfloat16)
    ahead = jnp.dot(before, choose.astype(jnp.bfloat16), preferred_element_type=jnp.float32)
    position = jnp.sum(jnp.where(choose, ahead, 0.0), axis=1).astype(jnp.int32)
    placed = (
        (target * capacity + position)[None, :] == jnp.arange(slots, dtype=jnp.int32)[:, None]
    ).astype(jnp.bfloat16)
    number = jnp.broadcast_to((opponent % per_owner + 1)[:, None], (rows, LANES))
    payload = jnp.concatenate([states, number.astype(jnp.bfloat16)], axis=1)
    send = jnp.dot(placed, payload, preferred_element_type=jnp.float32).astype(jnp.bfloat16)
    recv = lax.all_to_all(
        send.reshape(owners, capacity, width + LANES), TRUNK, 0, 0, tiled=True
    ).reshape(slots, width + LANES)

    mine, other = after((mine, other), send, up_far[0][2])
    gathered = lax.all_gather(jnp.concatenate([mine, other], axis=1), ("z", "c"), axis=0)

    up_far.append(swap(proj_up, 1, 3, recv))
    partial_rank = pl.pallas_call(
        down_kernel,
        out_shape=jax.ShapeDtypeStruct((n_adapter, 16, LANES), jnp.float32),
        in_specs=[VMEM_SPEC] * 2,
        out_specs=VMEM_SPEC,
        scratch_shapes=[pltpu.VMEM((slots, LANES), jnp.float32)],
        compiler_params=pltpu.CompilerParams(vmem_limit_bytes=14 * 2**20),
        cost_estimate=COST,
        name="down",
    )(recv, jnp.transpose(adapter_down, (0, 2, 1)).reshape(per_owner * rank, width))
    gate_far = [swap(proj_gate, first, 2, partial_rank) for first in (0, 2)]
    rank_parts = lax.all_to_all(partial_rank, ADAPTER, 0, 0, tiled=True)
    def finish(partial):
        return lax.psum_scatter(partial, "x", scatter_dimension=0, tiled=False).astype(jnp.float32)

    ups, done = multiply(gathered, proj_up, up_far, flags, rank_parts, gate_far[0][2])
    up_sum = finish(ups)
    rank_sum = pl.pallas_call(
        sum_kernel,
        out_shape=jax.ShapeDtypeStruct((n_adapter, 16, LANES), jnp.bfloat16),
        in_specs=[VMEM_SPEC] + [HBM_SPEC],
        out_specs=VMEM_SPEC,
        cost_estimate=COST,
        name="sum",
    )(rank_parts, done)
    rank_half = lax.all_to_all(rank_sum, ADAPTER, 0, 0, tiled=True)
    gates, done = multiply(gathered, proj_gate, gate_far, flags, rank_half)
    gate_sum = finish(gates)

    offsets = pl.pallas_call(
        up_kernel,
        out_shape=jax.ShapeDtypeStruct((slots, hidden), jnp.bfloat16),
        in_specs=[VMEM_SPEC] * 3 + [HBM_SPEC],
        out_specs=VMEM_SPEC,
        scratch_shapes=[
            pltpu.VMEM((slots, LANES), jnp.float32),
            pltpu.VMEM((slots // 3, per_owner * rank), jnp.bfloat16),
        ],
        compiler_params=pltpu.CompilerParams(vmem_limit_bytes=18 * 2**20),
        cost_estimate=COST,
        name="up",
    )(rank_half, recv, adapter_up.reshape(per_owner * rank, hidden), done)
    returned = lax.all_to_all(
        offsets.reshape(owners, capacity, hidden), TRUNK, 0, 0, tiled=True
    ).reshape(slots, hidden)
    offset = lax.dot_general(
        placed, returned, (((0,), (0,)), ((), ())), preferred_element_type=jnp.float32
    )
    return (jax.nn.silu(gate_sum + offset) * up_sum).astype(jnp.bfloat16)


def solution(mesh):
    fine = Mesh(mesh.devices.reshape(2, NX, NZ, 2, 2), TRUNK + ADAPTER)
    placed = (
        P(TRUNK, ADAPTER),
        P(TRUNK),
        P(TRUNK, ADAPTER),
        P(TRUNK, ADAPTER),
        P(TRUNK, ADAPTER, None),
        P(TRUNK, None, ADAPTER),
    )
    return jax.shard_map(
        on_device, mesh=fine, in_specs=placed, out_specs=P(TRUNK, ADAPTER), check_vma=False
    )
```

```python
import functools

import jax
import jax.numpy as jnp
from jax import lax
from jax.experimental import pallas as pl
from jax.experimental.pallas import tpu as pltpu
from jax.sharding import Mesh, PartitionSpec as P

TRUNK = ("yh", "x")
ADAPTER = ("z", "yl", "c")
SWAP = [(0, 1), (1, 0)]
NX, NZ = 4, 8
LANES = 128
NEAR = (0, 1, 2, -1)
HBM_SPEC = pl.BlockSpec(memory_space=pltpu.HBM)
VMEM_SPEC = pl.BlockSpec(memory_space=pltpu.VMEM)
COST = pl.CostEstimate(flops=8 * 10**9, bytes_accessed=16 * 2**20, transcendentals=0)


def after(value, *others):
    return lax.optimization_barrier((value, others))[0]


def start_pairs(flip):
    pairs = []
    for xs in range(NX):
        for h in range(2):
            for xd in range(NX):
                for yl in range(2):
                    z = h * NX + xd
                    to = (z + NEAR[(xs - xd) % NX]) % NZ
                    pairs.append(((xs * NZ + z) * 2 + yl, (xd * NZ + to) * 2 + (yl ^ flip)))
    return pairs


def multiply_kernel(pieces, flags, rows_ref, up_ref, gate_ref, *refs):
    far_refs = refs[: len(pieces)]
    out_ref, done_ref, lhs, rhs, out, lhs_sems, rhs_sems, out_sems = refs[-8:]
    yh, yl, here = flags[0], flags[1], flags[2]
    depth, hidden = up_ref.shape
    width = depth // 4
    chunks = []
    for matrix, ref in enumerate((up_ref, gate_ref)):
        chunks += [(ref, n * width, yh, matrix, n) for n in range(4)]
    for (matrix, first, count), ref in zip(pieces, far_refs):
        chunks += [(ref, n * width, 1 - yh, matrix, first + n) for n in range(count)]
    weights = []
    for n, (ref, at, block, matrix, source) in enumerate(chunks):
        y = jnp.where(yl == source // 2, 0, 1)
        to = pl.multiple_of(block * depth + (source % 2 * 2 + y) * width, width)
        weights.append(
            pltpu.make_async_copy(
                ref.at[pl.ds(at, width), :],
                rhs.at[pl.ds(to, width), pl.ds(matrix * hidden, hidden)],
                rhs_sems.at[n],
            )
        )
    rows, stores = [], []
    for n in range(NX):
        rows.append(
            [
                pltpu.make_async_copy(
                    rows_ref.at[lax.rem(h * NX + here + NEAR[n] + NZ, NZ) * 2 + core],
                    lhs.at[n, :, pl.ds((h * 2 + core) * 2 * width, 2 * width)],
                    lhs_sems.at[n, h * 2 + core],
                )
                for h in range(2)
                for core in range(2)
            ]
        )
        stores.append(
            pltpu.make_async_copy(out.at[n], out_ref.at[lax.rem(here + n, NX)], out_sems.at[n])
        )
    for copy in weights + rows[0] + rows[1]:
        copy.start()
    for copy in weights:
        copy.wait()
    for n in range(NX):
        for copy in rows[n]:
            copy.wait()
        if n + 2 < NX:
            for copy in rows[n + 2]:
                copy.start()
        out[n] = jnp.dot(lhs[n], rhs[...], preferred_element_type=jnp.float32).astype(
            jnp.bfloat16
        )
        stores[n].start()
    done_ref[...] = jnp.zeros_like(done_ref)
    for copy in stores:
        copy.wait()


def multiply(rows, proj_up, proj_gate, far, flags, *others):
    size = rows.shape[1]
    depth, hidden = proj_up.shape
    pieces = [piece[:3] for piece in far]
    return pl.pallas_call(
        functools.partial(multiply_kernel, pieces),
        out_shape=[
            jax.ShapeDtypeStruct((NX, size, 2 * hidden), jnp.bfloat16),
            jax.ShapeDtypeStruct((8, LANES), jnp.float32),
        ],
        in_specs=[pl.BlockSpec(memory_space=pltpu.SMEM)]
        + [HBM_SPEC] * (3 + len(far) + len(others)),
        out_specs=[HBM_SPEC, VMEM_SPEC],
        scratch_shapes=[
            pltpu.VMEM((NX, size, 2 * depth), jnp.bfloat16),
            pltpu.VMEM((2 * depth, 2 * hidden), jnp.bfloat16),
            pltpu.VMEM((NX, size, 2 * hidden), jnp.bfloat16),
            pltpu.SemaphoreType.DMA((NX, 4)),
            pltpu.SemaphoreType.DMA((16,)),
            pltpu.SemaphoreType.DMA((NX,)),
        ],
        compiler_params=pltpu.CompilerParams(vmem_limit_bytes=56 * 2**20),
        cost_estimate=COST,
        name="multiply",
    )(flags, rows, proj_up, proj_gate, *[piece[3] for piece in far], *others)


def names_of(recv_ref, tile, rows):
    return recv_ref[pl.ds(tile * rows, rows), 256:].astype(jnp.float32)


def opponent_of(lanes, first, rank):
    return (first + 1 + lax.broadcasted_iota(jnp.int32, (1, lanes), 1) // rank).astype(jnp.float32)


def down_kernel(recv_ref, down_ref, _, out_ref, total):
    slots, rank, width = recv_ref.shape[0], 64, 256
    tiles = 3
    rows = slots // tiles
    total[...] = jnp.zeros_like(total)

    def step(chunk, carry):
        maps = down_ref[pl.ds(pl.multiple_of(chunk * 4 * rank, 4 * rank), 4 * rank), :]
        for tile in range(tiles):
            at = pl.ds(tile * rows, rows)
            product = lax.dot_general(
                recv_ref[at, :width], maps, (((1,), (1,)), ((), ())),
                preferred_element_type=jnp.float32,
            )
            names = names_of(recv_ref, tile, rows)
            first = names == opponent_of(LANES, chunk * 4, rank)
            second = names == opponent_of(LANES, chunk * 4 + 2, rank)
            total[at, :] += jnp.where(first, product[:, :LANES], 0.0) + jnp.where(
                second, product[:, LANES:], 0.0
            )
        return carry

    lax.fori_loop(0, down_ref.shape[0] // (4 * rank), step, 0)
    both = total[...] + pltpu.roll(total[...], rank, 1)
    n = out_ref.shape[0]
    low = both[: 16 * n].reshape(n, 16, LANES)
    high = both[16 * n :].reshape(n, 8, LANES)
    left = lax.broadcasted_iota(jnp.int32, (1, 1, LANES), 2) < rank
    out_ref[:, :8, :] = jnp.where(left, low[:, :8], high)
    out_ref[:, 8:, :] = jnp.where(left, low[:, 8:], 0.0)


def sum_kernel(parts_ref, *refs):
    out_ref = refs[-1]
    total = jnp.sum(parts_ref[...], axis=0).astype(jnp.bfloat16)
    out_ref[...] = jnp.broadcast_to(total[None], out_ref.shape)


def up_kernel(rank_ref, recv_ref, up_ref, *refs):
    out_ref, whole, spread = refs[-3:]
    slots, rank = recv_ref.shape[0], 64
    n = rank_ref.shape[0]
    packed = rank_ref[...].astype(jnp.float32)
    left = lax.broadcasted_iota(jnp.int32, (1, LANES), 1) < rank
    low = packed.reshape(n * 16, LANES)
    high = packed[:, :8].reshape(n * 8, LANES)
    whole[: n * 16, :] = jnp.where(left, low, pltpu.roll(low, rank, 1))
    whole[n * 16 :, :] = jnp.where(left, pltpu.roll(high, rank, 1), high)
    tiles = 3
    rows = slots // tiles

    def step(tile, carry):
        at = pl.ds(pl.multiple_of(tile * rows, rows), rows)
        names = recv_ref[at, 256:].astype(jnp.float32)
        values = whole[at, :]
        for pair in range(up_ref.shape[0] // LANES):
            mine = names == opponent_of(LANES, pair * 2, rank)
            spread[:, pair * LANES : (pair + 1) * LANES] = jnp.where(mine, values, 0.0).astype(
                jnp.bfloat16
            )
        out_ref[at, :] = jnp.dot(
            spread[...], up_ref[...], preferred_element_type=jnp.float32
        ).astype(out_ref.dtype)
        return carry

    lax.fori_loop(0, tiles, step, 0)


def on_device(states, opponent, proj_gate, proj_up, adapter_down, adapter_up):
    rows, width = states.shape
    hidden = proj_gate.shape[1]
    owners = lax.axis_size(TRUNK)
    n_adapter = lax.axis_size(ADAPTER)
    per_owner, _, rank = adapter_down.shape
    capacity = 2 * rows // owners
    slots = owners * capacity
    flags = jnp.stack([lax.axis_index(name) for name in ("yh", "yl", "x")]).astype(jnp.int32)

    mine = lax.ppermute(states, ("x", "z", "yl"), start_pairs(0))
    other = lax.ppermute(states, ("x", "z", "yl"), start_pairs(1))
    quarter = proj_up.shape[0] // 4

    def swap(matrix, first, count):
        part = (proj_up, proj_gate)[matrix][first * quarter : (first + count) * quarter]
        return matrix, first, count, lax.ppermute(part, "yh", SWAP)

    far = [swap(0, 0, 2), swap(0, 2, 2), swap(1, 0, 2), swap(1, 2, 2)]

    target = opponent // per_owner
    choose = target[:, None] == jnp.arange(owners, dtype=jnp.int32)[None, :]
    count = jnp.arange(rows, dtype=jnp.int32)
    before = (count[:, None] > count[None, :]).astype(jnp.bfloat16)
    ahead = jnp.dot(before, choose.astype(jnp.bfloat16), preferred_element_type=jnp.float32)
    position = jnp.sum(jnp.where(choose, ahead, 0.0), axis=1).astype(jnp.int32)
    placed = (
        (target * capacity + position)[None, :] == jnp.arange(slots, dtype=jnp.int32)[:, None]
    ).astype(jnp.bfloat16)
    number = jnp.broadcast_to((opponent % per_owner + 1)[:, None], (rows, LANES))
    payload = jnp.concatenate([states, number.astype(jnp.bfloat16)], axis=1)
    send = jnp.dot(placed, payload, preferred_element_type=jnp.float32).astype(jnp.bfloat16)
    recv = lax.all_to_all(
        send.reshape(owners, capacity, width + LANES), TRUNK, 0, 0, tiled=True
    ).reshape(slots, width + LANES)

    mine, other = after((mine, other), send, far[0][3])
    gathered = lax.all_gather(jnp.concatenate([mine, other], axis=1), ("z", "c"), axis=0)

    partial_rank = pl.pallas_call(
        down_kernel,
        out_shape=jax.ShapeDtypeStruct((n_adapter, 16, LANES), jnp.float32),
        in_specs=[VMEM_SPEC] * 2 + [HBM_SPEC],
        out_specs=VMEM_SPEC,
        scratch_shapes=[pltpu.VMEM((slots, LANES), jnp.float32)],
        compiler_params=pltpu.CompilerParams(vmem_limit_bytes=14 * 2**20),
        cost_estimate=COST,
        name="down",
    )(recv, jnp.transpose(adapter_down, (0, 2, 1)).reshape(per_owner * rank, width), far[1][3])
    rank_parts = lax.all_to_all(partial_rank, ADAPTER, 0, 0, tiled=True)
    partial, done = multiply(gathered, proj_up, proj_gate, far, flags, rank_parts)
    total = lax.psum_scatter(partial, "x", scatter_dimension=0, tiled=False)
    rank_sum = pl.pallas_call(
        sum_kernel,
        out_shape=jax.ShapeDtypeStruct((n_adapter, 16, LANES), jnp.bfloat16),
        in_specs=[VMEM_SPEC, HBM_SPEC],
        out_specs=VMEM_SPEC,
        cost_estimate=COST,
        name="sum",
    )(rank_parts, done)
    rank_half = lax.all_to_all(rank_sum, ADAPTER, 0, 0, tiled=True)

    offsets = pl.pallas_call(
        up_kernel,
        out_shape=jax.ShapeDtypeStruct((slots, hidden), jnp.bfloat16),
        in_specs=[VMEM_SPEC] * 3 + [HBM_SPEC],
        out_specs=VMEM_SPEC,
        scratch_shapes=[
            pltpu.VMEM((slots, LANES), jnp.float32),
            pltpu.VMEM((slots // 3, per_owner * rank), jnp.bfloat16),
        ],
        compiler_params=pltpu.CompilerParams(vmem_limit_bytes=18 * 2**20),
        cost_estimate=COST,
        name="up",
    )(rank_half, recv, adapter_up.reshape(per_owner * rank, hidden), done)
    returned = lax.all_to_all(
        offsets.reshape(owners, capacity, hidden), TRUNK, 0, 0, tiled=True
    ).reshape(slots, hidden)
    offset = lax.dot_general(
        placed, returned, (((0,), (0,)), ((), ())), preferred_element_type=jnp.float32
    )
    up_sum, gate_sum = total[:, :hidden], total[:, hidden:]
    gate = gate_sum.astype(jnp.float32) + offset
    return (jax.nn.silu(gate) * up_sum.astype(jnp.float32)).astype(jnp.bfloat16)


def solution(mesh):
    fine = Mesh(mesh.devices.reshape(2, NX, NZ, 2, 2), TRUNK + ADAPTER)
    placed = (
        P(TRUNK, ADAPTER),
        P(TRUNK),
        P(TRUNK, ADAPTER),
        P(TRUNK, ADAPTER),
        P(TRUNK, ADAPTER, None),
        P(TRUNK, None, ADAPTER),
    )
    return jax.shard_map(
        on_device, mesh=fine, in_specs=placed, out_specs=P(TRUNK, ADAPTER), check_vma=False
    )
```

```python
import functools

import jax
import jax.numpy as jnp
from jax import lax
from jax.experimental import pallas as pl
from jax.experimental.pallas import tpu as pltpu
from jax.sharding import Mesh, PartitionSpec as P

TRUNK = ("yh", "x")
ADAPTER = ("z", "yl", "c")
SWAP = [(0, 1), (1, 0)]
NX, NZ = 4, 8
LANES = 128
NEAR = (0, 1, 2, -1)
HBM_SPEC = pl.BlockSpec(memory_space=pltpu.HBM)
VMEM_SPEC = pl.BlockSpec(memory_space=pltpu.VMEM)
COST = pl.CostEstimate(flops=8 * 10**9, bytes_accessed=16 * 2**20, transcendentals=0)


def after(value, *others):
    return lax.optimization_barrier((value, others))[0]


def start_pairs(flip):
    pairs = []
    for xs in range(NX):
        for h in range(2):
            for xd in range(NX):
                for yl in range(2):
                    z = h * NX + xd
                    to = (z + NEAR[(xs - xd) % NX]) % NZ
                    pairs.append(((xs * NZ + z) * 2 + yl, (xd * NZ + to) * 2 + (yl ^ flip)))
    return pairs


def multiply_kernel(pieces, flags, rows_ref, up_ref, gate_ref, *refs):
    far_refs = refs[: len(pieces)]
    out_ref, done_ref, lhs, rhs, out, lhs_sems, rhs_sems, out_sems = refs[-8:]
    yh, yl, here = flags[0], flags[1], flags[2]
    depth, hidden = up_ref.shape
    width = depth // 4
    chunks = []
    for matrix, ref in enumerate((up_ref, gate_ref)):
        chunks += [(ref, n * width, yh, matrix, n) for n in range(4)]
    for (matrix, first, count), ref in zip(pieces, far_refs):
        chunks += [(ref, n * width, 1 - yh, matrix, first + n) for n in range(count)]
    weights = []
    for n, (ref, at, block, matrix, source) in enumerate(chunks):
        y = jnp.where(yl == source // 2, 0, 1)
        to = pl.multiple_of(block * depth + (source % 2 * 2 + y) * width, width)
        weights.append(
            pltpu.make_async_copy(
                ref.at[pl.ds(at, width), :],
                rhs.at[pl.ds(to, width), pl.ds(matrix * hidden, hidden)],
                rhs_sems.at[n],
            )
        )
    rows, stores = [], []
    for n in range(NX):
        rows.append(
            [
                pltpu.make_async_copy(
                    rows_ref.at[lax.rem(h * NX + here + NEAR[n] + NZ, NZ) * 2 + core],
                    lhs.at[n, :, pl.ds((h * 2 + core) * 2 * width, 2 * width)],
                    lhs_sems.at[n, h * 2 + core],
                )
                for h in range(2)
                for core in range(2)
            ]
        )
        stores.append(
            pltpu.make_async_copy(out.at[n], out_ref.at[lax.rem(here + n, NX)], out_sems.at[n])
        )
    for copy in weights + rows[0]:
        copy.start()
    for copy in weights:
        copy.wait()
    for n in range(NX):
        for copy in rows[n]:
            copy.wait()
        if n + 1 < NX:
            for copy in rows[n + 1]:
                copy.start()
        out[n] = jnp.dot(lhs[n], rhs[...], preferred_element_type=jnp.float32).astype(
            jnp.bfloat16
        )
        stores[n].start()
    done_ref[...] = jnp.zeros_like(done_ref)
    for copy in stores:
        copy.wait()


def multiply(rows, proj_up, proj_gate, far, flags, *others):
    size = rows.shape[1]
    depth, hidden = proj_up.shape
    pieces = [piece[:3] for piece in far]
    return pl.pallas_call(
        functools.partial(multiply_kernel, pieces),
        out_shape=[
            jax.ShapeDtypeStruct((NX, size, 2 * hidden), jnp.bfloat16),
            jax.ShapeDtypeStruct((8, LANES), jnp.float32),
        ],
        in_specs=[pl.BlockSpec(memory_space=pltpu.SMEM)]
        + [HBM_SPEC] * (3 + len(far) + len(others)),
        out_specs=[HBM_SPEC, VMEM_SPEC],
        scratch_shapes=[
            pltpu.VMEM((NX, size, 2 * depth), jnp.bfloat16),
            pltpu.VMEM((2 * depth, 2 * hidden), jnp.bfloat16),
            pltpu.VMEM((NX, size, 2 * hidden), jnp.bfloat16),
            pltpu.SemaphoreType.DMA((NX, 4)),
            pltpu.SemaphoreType.DMA((16,)),
            pltpu.SemaphoreType.DMA((NX,)),
        ],
        compiler_params=pltpu.CompilerParams(vmem_limit_bytes=56 * 2**20),
        cost_estimate=COST,
        name="multiply",
    )(flags, rows, proj_up, proj_gate, *[piece[3] for piece in far], *others)


def names_of(recv_ref, tile, rows):
    return recv_ref[pl.ds(tile * rows, rows), 256:].astype(jnp.float32)


def opponent_of(lanes, first, rank):
    return (first + 1 + lax.broadcasted_iota(jnp.int32, (1, lanes), 1) // rank).astype(jnp.float32)


def down_kernel(recv_ref, down_ref, _, out_ref, total):
    slots, rank, width = recv_ref.shape[0], 64, 256
    tiles = 3
    rows = slots // tiles
    total[...] = jnp.zeros_like(total)

    def step(chunk, carry):
        maps = down_ref[pl.ds(pl.multiple_of(chunk * 4 * rank, 4 * rank), 4 * rank), :]
        for tile in range(tiles):
            at = pl.ds(tile * rows, rows)
            product = lax.dot_general(
                recv_ref[at, :width], maps, (((1,), (1,)), ((), ())),
                preferred_element_type=jnp.float32,
            )
            names = names_of(recv_ref, tile, rows)
            first = names == opponent_of(LANES, chunk * 4, rank)
            second = names == opponent_of(LANES, chunk * 4 + 2, rank)
            total[at, :] += jnp.where(first, product[:, :LANES], 0.0) + jnp.where(
                second, product[:, LANES:], 0.0
            )
        return carry

    lax.fori_loop(0, down_ref.shape[0] // (4 * rank), step, 0)
    both = total[...] + pltpu.roll(total[...], rank, 1)
    n = out_ref.shape[0]
    low = both[: 16 * n].reshape(n, 16, LANES)
    high = both[16 * n :].reshape(n, 8, LANES)
    left = lax.broadcasted_iota(jnp.int32, (1, 1, LANES), 2) < rank
    out_ref[:, :8, :] = jnp.where(left, low[:, :8], high)
    out_ref[:, 8:, :] = jnp.where(left, low[:, 8:], 0.0)


def sum_kernel(parts_ref, *refs):
    out_ref = refs[-1]
    total = jnp.sum(parts_ref[...], axis=0).astype(jnp.bfloat16)
    out_ref[...] = jnp.broadcast_to(total[None], out_ref.shape)


def up_kernel(rank_ref, recv_ref, up_ref, *refs):
    out_ref, whole, spread = refs[-3:]
    slots, rank = recv_ref.shape[0], 64
    n = rank_ref.shape[0]
    packed = rank_ref[...].astype(jnp.float32)
    left = lax.broadcasted_iota(jnp.int32, (1, LANES), 1) < rank
    low = packed.reshape(n * 16, LANES)
    high = packed[:, :8].reshape(n * 8, LANES)
    whole[: n * 16, :] = jnp.where(left, low, pltpu.roll(low, rank, 1))
    whole[n * 16 :, :] = jnp.where(left, pltpu.roll(high, rank, 1), high)
    tiles = 3
    rows = slots // tiles

    def step(tile, carry):
        at = pl.ds(pl.multiple_of(tile * rows, rows), rows)
        names = recv_ref[at, 256:].astype(jnp.float32)
        values = whole[at, :]
        for pair in range(up_ref.shape[0] // LANES):
            mine = names == opponent_of(LANES, pair * 2, rank)
            spread[:, pair * LANES : (pair + 1) * LANES] = jnp.where(mine, values, 0.0).astype(
                jnp.bfloat16
            )
        out_ref[at, :] = jnp.dot(
            spread[...], up_ref[...], preferred_element_type=jnp.float32
        ).astype(out_ref.dtype)
        return carry

    lax.fori_loop(0, tiles, step, 0)


def on_device(states, opponent, proj_gate, proj_up, adapter_down, adapter_up):
    rows, width = states.shape
    hidden = proj_gate.shape[1]
    owners = lax.axis_size(TRUNK)
    n_adapter = lax.axis_size(ADAPTER)
    per_owner, _, rank = adapter_down.shape
    capacity = 2 * rows // owners
    slots = owners * capacity
    flags = jnp.stack([lax.axis_index(name) for name in ("yh", "yl", "x")]).astype(jnp.int32)

    mine = lax.ppermute(states, ("x", "z", "yl"), start_pairs(0))
    other = lax.ppermute(states, ("x", "z", "yl"), start_pairs(1))
    quarter = proj_up.shape[0] // 4

    def swap(matrix, first, count):
        part = (proj_up, proj_gate)[matrix][first * quarter : (first + count) * quarter]
        return matrix, first, count, lax.ppermute(part, "yh", SWAP)

    far = [swap(0, 0, 1), swap(0, 1, 3), swap(1, 0, 2), swap(1, 2, 2)]

    target = opponent // per_owner
    choose = target[:, None] == jnp.arange(owners, dtype=jnp.int32)[None, :]
    count = jnp.arange(rows, dtype=jnp.int32)
    before = (count[:, None] > count[None, :]).astype(jnp.bfloat16)
    ahead = jnp.dot(before, choose.astype(jnp.bfloat16), preferred_element_type=jnp.float32)
    position = jnp.sum(jnp.where(choose, ahead, 0.0), axis=1).astype(jnp.int32)
    placed = (
        (target * capacity + position)[None, :] == jnp.arange(slots, dtype=jnp.int32)[:, None]
    ).astype(jnp.bfloat16)
    number = jnp.broadcast_to((opponent % per_owner + 1)[:, None], (rows, LANES))
    payload = jnp.concatenate([states, number.astype(jnp.bfloat16)], axis=1)
    send = jnp.dot(placed, payload, preferred_element_type=jnp.float32).astype(jnp.bfloat16)
    recv = lax.all_to_all(
        send.reshape(owners, capacity, width + LANES), TRUNK, 0, 0, tiled=True
    ).reshape(slots, width + LANES)

    mine, other = after((mine, other), send, far[0][3])
    gathered = lax.all_gather(jnp.concatenate([mine, other], axis=1), ("z", "c"), axis=0)

    partial_rank = pl.pallas_call(
        down_kernel,
        out_shape=jax.ShapeDtypeStruct((n_adapter, 16, LANES), jnp.float32),
        in_specs=[VMEM_SPEC] * 2 + [HBM_SPEC],
        out_specs=VMEM_SPEC,
        scratch_shapes=[pltpu.VMEM((slots, LANES), jnp.float32)],
        compiler_params=pltpu.CompilerParams(vmem_limit_bytes=14 * 2**20),
        cost_estimate=COST,
        name="down",
    )(recv, jnp.transpose(adapter_down, (0, 2, 1)).reshape(per_owner * rank, width), far[1][3])
    rank_parts = lax.all_to_all(partial_rank, ADAPTER, 0, 0, tiled=True)
    partial, done = multiply(gathered, proj_up, proj_gate, far, flags, rank_parts)
    total = lax.psum_scatter(partial, "x", scatter_dimension=0, tiled=False)
    rank_sum = pl.pallas_call(
        sum_kernel,
        out_shape=jax.ShapeDtypeStruct((n_adapter, 16, LANES), jnp.bfloat16),
        in_specs=[VMEM_SPEC, HBM_SPEC],
        out_specs=VMEM_SPEC,
        cost_estimate=COST,
        name="sum",
    )(rank_parts, done)
    rank_half = lax.all_to_all(rank_sum, ADAPTER, 0, 0, tiled=True)

    offsets = pl.pallas_call(
        up_kernel,
        out_shape=jax.ShapeDtypeStruct((slots, hidden), jnp.bfloat16),
        in_specs=[VMEM_SPEC] * 3 + [HBM_SPEC],
        out_specs=VMEM_SPEC,
        scratch_shapes=[
            pltpu.VMEM((slots, LANES), jnp.float32),
            pltpu.VMEM((slots // 3, per_owner * rank), jnp.bfloat16),
        ],
        compiler_params=pltpu.CompilerParams(vmem_limit_bytes=18 * 2**20),
        cost_estimate=COST,
        name="up",
    )(rank_half, recv, adapter_up.reshape(per_owner * rank, hidden), done)
    returned = lax.all_to_all(
        offsets.reshape(owners, capacity, hidden), TRUNK, 0, 0, tiled=True
    ).reshape(slots, hidden)
    offset = lax.dot_general(
        placed, returned, (((0,), (0,)), ((), ())), preferred_element_type=jnp.float32
    )
    up_sum, gate_sum = total[:, :hidden], total[:, hidden:]
    gate = gate_sum.astype(jnp.float32) + offset
    return (jax.nn.silu(gate) * up_sum.astype(jnp.float32)).astype(jnp.bfloat16)


def solution(mesh):
    fine = Mesh(mesh.devices.reshape(2, NX, NZ, 2, 2), TRUNK + ADAPTER)
    placed = (
        P(TRUNK, ADAPTER),
        P(TRUNK),
        P(TRUNK, ADAPTER),
        P(TRUNK, ADAPTER),
        P(TRUNK, ADAPTER, None),
        P(TRUNK, None, ADAPTER),
    )
    return jax.shard_map(
        on_device, mesh=fine, in_specs=placed, out_specs=P(TRUNK, ADAPTER), check_vma=False
    )
```
